256 devices in a mesh: frame: 8 (over z), height: 16 (over x, y), head: 2 (over core).
Axes of the slice: x: 4, y: 4, z: 8, core: 2. Of those that a mesh axis runs over, the one named last changes fastest.
Arguments:
- q_raw: bfloat16 [16, 48, 80, 5120], P('frame', 'height', None, 'head'), may hold values from -8 to 8
- k_raw: bfloat16 [16, 48, 80, 5120], P('frame', 'height', None, 'head'), may hold values from -8 to 8
- v_in: bfloat16 [16, 48, 80, 5120], P('frame', 'height', None, 'head'), may hold values from -6 to 6
- q_gain: float32 [5120], P('head'), may hold values from 0.8 to 2
- k_gain: float32 [5120], P('head'), may hold values from 0.8 to 2
- window: int32 [40, 3], P('head'), may hold values from 0 to 9, as said below
Outputs:
- attended: bfloat16 [16, 48, 80, 5120], P('frame', 'height', None, 'head')
The draws below stay inside these ranges and needn't reach their ends.
Inputs may be any that keep to these rules, and one draw needn't show every extreme that they name: window[h, 0] and window[h, 1] are 0 or 1, window[h, 2] lies in 0 to 9; some head has (1, 1, 9).
All inputs are finite; a program needn't handle non-finite values.
Results may differ from the reference program's by a relative error of at most 0.012.
Values may be sent and summed in bfloat16 or wider, within the bound.
No kernel may reach another device: no remote copies, remote signals or barrier semaphores. Data moves between devices by JAX's collectives and lax.ppermute only.
A program may use at most 128 MiB of HBM per device.

```python
import math
import jax
import jax.numpy as jnp
from jax import lax

HEADS = 40
HD = 128
D = 5120
W = 80
TILE_W = 8
COL_TILES = 10
FRAMES = 16
ROWS = 48


def draw_q_raw(key, part):
    key = jax.random.fold_in(key, 11)
    first_key = jax.random.fold_in(key, 0)
    shape = (FRAMES * ROWS * W, HEADS, HD)
    values = jnp.clip(jax.random.normal(first_key, shape), -4.0, 4.0)
    return values.reshape(FRAMES, ROWS, W, HEADS * HD).astype(jnp.bfloat16)


def draw_k_raw(key, part):
    key = jax.random.fold_in(key, 23)
    first_key = jax.random.fold_in(key, 0)
    shape = (FRAMES * ROWS * W, HEADS, HD)
    values = jnp.clip(jax.random.normal(first_key, shape), -4.0, 4.0)
    return values.reshape(FRAMES, ROWS, W, HEADS * HD).astype(jnp.bfloat16)


def draw_window(key, part):
    key = jax.random.fold_in(key, 37)
    parts_keys = jax.random.split(key, 4)
    frame_reach = (jax.random.randint(parts_keys[0], (HEADS,), 0, 4) > 0).astype(jnp.int32)
    row_reach = (jax.random.randint(parts_keys[1], (HEADS,), 0, 4) > 0).astype(jnp.int32)
    column_reach = jax.random.randint(parts_keys[2], (HEADS,), 0, COL_TILES)
    forced_head = jax.random.randint(parts_keys[3], (), 0, HEADS)
    chosen = jnp.arange(HEADS) == forced_head
    frame_reach = jnp.where(chosen, 1, frame_reach)
    row_reach = jnp.where(chosen, 1, row_reach)
    column_reach = jnp.where(chosen, COL_TILES - 1, column_reach)
    return jnp.stack((frame_reach, row_reach, column_reach), axis=1).astype(jnp.int32)


def steps_of(rng, extent, cuts, low, high):
    level = 1.0
    for dim, shards_of in cuts:
        draws = jax.random.uniform(jax.random.fold_in(jax.random.fold_in(rng, 6), dim), (shards_of,), jnp.float32, low / len(cuts), high / len(cuts))
        level = level * jnp.repeat(jnp.exp(draws), extent[dim] // shards_of).reshape((-1,) + (1,) * (len(extent) - 1 - dim))
    return level


def normal_values(rng, extent, spread, reach, cuts=(), kind=jnp.bfloat16):
    result = jax.random.normal(rng, extent, jnp.float32) * spread
    if len(cuts) > 0:
        result = steps_of(rng, extent, cuts, -0.22, 0.18) * result
    return jnp.clip(result, min=-reach, max=reach).astype(kind)


def setup_inputs(seed: int = 0) -> dict:
    streams_of = jax.random.split(jax.random.key(seed), 7)
    q_raw = draw_q_raw(jax.random.fold_in(streams_of[6], 71), 0)
    k_raw = draw_k_raw(jax.random.fold_in(streams_of[6], 71), 0)
    v_in = normal_values(streams_of[2], (FRAMES, ROWS, W, D), 1.0, 6.0, ((0, 8), (1, 16), (3, 2)))
    q_gain = jnp.clip(jnp.exp(math.log(2.0) - 0.9162907 * jax.random.uniform(streams_of[3], (D,), jnp.float32) ** steps_of(streams_of[3], (D,), ((0, 2),), -0.2, 0.2)), 0.8, 2.0)
    k_gain = jnp.clip(jnp.exp(math.log(2.0) - 0.9162907 * jax.random.uniform(streams_of[4], (D,), jnp.float32) ** steps_of(streams_of[4], (D,), ((0, 2),), -0.2, 0.2)), 0.8, 2.0)
    window = draw_window(jax.random.fold_in(streams_of[6], 71), 0)
    return {"q_raw": q_raw, "k_raw": k_raw, "v_in": v_in, "q_gain": q_gain, "k_gain": k_gain, "window": window}


epsilon_norm = 1e-06

def normalize(raw, gain):
    values = raw.astype(jnp.float32)
    square_sum = lax.optimization_barrier(jnp.sum(values * values, axis=-1, keepdims=True))
    inverse = lax.rsqrt(square_sum / values.shape[-1] + epsilon_norm)
    return (values * inverse * gain).astype(jnp.bfloat16)

def reference(q_raw, k_raw, v_in, q_gain, k_gain, window):
    frame_count, row_count, width_cols, channels = q_raw.shape
    query_norm = lax.map(lambda slab: normalize(slab, q_gain), q_raw)
    key_norm = lax.map(lambda slab: normalize(slab, k_gain), k_raw)
    padding = ((1, 1), (1, 1), (0, 0), (0, 0))
    key_padded = jnp.pad(key_norm, padding)
    value_padded = jnp.pad(v_in, padding)
    key_count = 9 * width_cols
    key_ids = jnp.arange(key_count, dtype=jnp.int32)
    frame_offset = key_ids // (3 * width_cols) - 1
    row_offset = key_ids // width_cols % 3 - 1
    key_column = key_ids % width_cols
    query_column = jnp.arange(width_cols, dtype=jnp.int32)
    tile_gap = jnp.abs(query_column[:, None] // TILE_W - key_column[None, :] // TILE_W)
    score_scale = HD ** (-0.5)
    zero_index = jnp.zeros((), jnp.int32)

    def attend_row(position):
        frame_at = (position // row_count).astype(jnp.int32)
        row_at = (position % row_count).astype(jnp.int32)
        query_block = lax.dynamic_slice(query_norm, (frame_at, row_at, zero_index, zero_index), (1, 1, width_cols, channels))
        query_block = query_block.reshape(width_cols, HEADS, HD).astype(jnp.float32)
        key_block = lax.dynamic_slice(key_padded, (frame_at, row_at, zero_index, zero_index), (3, 3, width_cols, channels))
        key_block = key_block.reshape(key_count, HEADS, HD).astype(jnp.float32)
        value_block = lax.dynamic_slice(value_padded, (frame_at, row_at, zero_index, zero_index), (3, 3, width_cols, channels))
        value_block = value_block.reshape(key_count, HEADS, HD).astype(jnp.float32)
        key_frame = frame_at + frame_offset
        key_row = row_at + row_offset
        key_valid = (key_frame >= 0) & (key_frame < frame_count) & (key_row >= 0) & (key_row < row_count)
        visible = jnp.abs(frame_offset)[None, None, :] <= window[:, 0][:, None, None]
        visible = visible & (jnp.abs(row_offset)[None, None, :] <= window[:, 1][:, None, None])
        visible = visible & (tile_gap[None, :, :] <= window[:, 2][:, None, None])
        visible = visible & key_valid[None, None, :]
        scores = jnp.einsum('qhd,khd->hqk', query_block, key_block) * score_scale
        scores = jnp.where(visible, scores, -jnp.inf)
        row_max = lax.optimization_barrier(jnp.max(scores, axis=-1, keepdims=True))
        weights = jnp.exp(scores - row_max)
        denominator = lax.optimization_barrier(jnp.sum(weights, axis=-1, keepdims=True))
        rounded_weights = weights.astype(jnp.bfloat16).astype(jnp.float32)
        mixed = jnp.einsum('hqk,khd->qhd', rounded_weights, value_block)
        mixed = mixed / jnp.transpose(denominator, (1, 0, 2))
        return mixed.astype(jnp.bfloat16).reshape(width_cols, channels)
    rows_out = lax.map(attend_row, jnp.arange(frame_count * row_count, dtype=jnp.int32))
    return rows_out.reshape(frame_count, row_count, width_cols, channels)
```

```python
import functools
import math

import jax
import jax.numpy as jnp
from jax import lax
from jax.experimental import pallas as pl
from jax.experimental.pallas import tpu as pltpu
from jax.sharding import PartitionSpec as P

HD = 128
W = 80
EPS = 1e-06
NEG = -1e30
LOG2E = math.log2(math.e)
SCALE2 = LOG2E / math.sqrt(HD)
F32 = jnp.float32
BF16 = jnp.bfloat16

NH = 20
AT_P = 0
AT_Y = NH
AT_PLACE = 2 * NH
AT_WIN = 3 * NH
AT_ROW_LO = 6 * NH
AT_ROW_HI = 6 * NH + 1
AT_FRAME_LO = 6 * NH + 2
AT_FRAME_HI = 6 * NH + 3
AT_NF = 6 * NH + 4


def params(mib=12):
    return pltpu.CompilerParams(vmem_limit_bytes=mib * 1024 * 1024)


def estimate(heads, pairs):
    flops = heads * pairs * HD * 4
    return pl.CostEstimate(flops=flops * 3, bytes_accessed=heads * 1_000_000, transcendentals=heads * pairs)


def normed(raw, inverse, gain):
    return (raw.astype(F32) * inverse * gain).astype(BF16)


def pack_queries_kernel(group, meta, *refs):
    raws = refs[:group]
    gains = refs[group : 2 * group]
    inverse, up, down = refs[2 * group :]
    for j in range(group):
        q = normed(raws[j][...], inverse[...], gains[j][...].reshape(1, 1, 1, HD))
        up[j] = q[1].reshape(3 * W, HD)
        down[j] = q[0].reshape(3 * W, HD)


def pack_rows_kernel(group, meta, *refs):
    keys = refs[:group]
    values = refs[group : 2 * group]
    gains = refs[2 * group : 3 * group]
    inverse, up, down = refs[3 * group :]
    for j in range(group):
        gain = gains[j][...].reshape(1, 1, HD)
        up[j, 0] = normed(keys[j][:, 2], inverse[:, 2], gain)
        up[j, 1] = values[j][:, 2]
        down[j, 0] = normed(keys[j][:, 0], inverse[:, 0], gain)
        down[j, 1] = values[j][:, 0]


def head_spec(at, start, group, j):
    return pl.BlockSpec((2, 3, W, HD), lambda s, meta: (0, 0, 0, meta[at + start + s * group + j]))


def gain_spec(at, start, group, j):
    return pl.BlockSpec((1, HD), lambda s, meta: (0, meta[at + start + s * group + j]))


def whole(shape):
    return pl.BlockSpec(shape, lambda s, meta: (0,) * len(shape))


def group_of(count):
    return 4 if count % 4 == 0 else 2


def pack_queries(meta, q, gain, inverse, count):
    group = group_of(count)
    out = jax.ShapeDtypeStruct((count, 3 * W, HD), BF16)
    out_spec = pl.BlockSpec((group, 3 * W, HD), lambda s, meta: (s, 0, 0))
    return pl.pallas_call(
        functools.partial(pack_queries_kernel, group),
        grid_spec=pltpu.PrefetchScalarGridSpec(
            num_scalar_prefetch=1,
            grid=(count // group,),
            in_specs=[head_spec(AT_P, 0, group, j) for j in range(group)]
            + [gain_spec(AT_P, 0, group, j) for j in range(group)]
            + [whole((2, 3, W, HD))],
            out_specs=[out_spec, out_spec],
        ),
        out_shape=[out, out],
        compiler_params=params(),
        cost_estimate=pl.CostEstimate(flops=count * 200_000, bytes_accessed=count * 250_000, transcendentals=0),
        name="pack_queries",
    )(meta, *([q] * group), *([gain] * group), inverse)


def pack_rows(meta, k, v, gain, inverse, start, count):
    group = group_of(count)
    out = jax.ShapeDtypeStruct((count, 2, 2, W, HD), BF16)
    out_spec = pl.BlockSpec((group, 2, 2, W, HD), lambda s, meta: (s, 0, 0, 0, 0))
    return pl.pallas_call(
        functools.partial(pack_rows_kernel, group),
        grid_spec=pltpu.PrefetchScalarGridSpec(
            num_scalar_prefetch=1,
            grid=(count // group,),
            in_specs=[head_spec(AT_Y, start, group, j) for j in range(group)] * 2
            + [gain_spec(AT_Y, start, group, j) for j in range(group)]
            + [whole((2, 3, W, HD))],
            out_specs=[out_spec, out_spec],
        ),
        out_shape=[out, out],
        compiler_params=params(),
        cost_estimate=pl.CostEstimate(flops=count * 200_000, bytes_accessed=count * 400_000, transcendentals=0),
        name="pack_rows",
    )(meta, *([k] * group), *([v] * group), *([gain] * group), inverse)


def fill_lines(kx, vx, k, v, inverse, gain, low, high):
    kn = normed(k[...], inverse[...], gain[...].reshape(1, 1, 1, HD))
    for j in range(2):
        kx[j, 0:W] = low[0, 0, j]
        kx[j, W : 4 * W] = kn[j].reshape(3 * W, HD)
        kx[j, 4 * W : 5 * W] = high[0, 0, j]
        vx[j, 0:W, 0:HD] = low[0, 1, j]
        vx[j, W : 4 * W, 0:HD] = v[j].reshape(3 * W, HD)
        vx[j, 4 * W : 5 * W, 0:HD] = high[0, 1, j]


def line_scratch(group):
    return [pltpu.VMEM((2, 5 * W, HD), BF16)] * group + [pltpu.VMEM((2, 5 * W, 2 * HD), BF16)] * group


def fill_ones(values):
    for vx in values:
        vx[:, :, HD:] = jnp.ones((2, 5 * W, HD), BF16)


def biases(meta, head):
    lane = lax.broadcasted_iota(jnp.int32, (W, 3 * W), 1)
    line = (lane >= W).astype(jnp.int32) + (lane >= 2 * W).astype(jnp.int32)
    key_tile = (lane - W * line) >> 3
    query_tile = lax.broadcasted_iota(jnp.int32, (W, 3 * W), 0) >> 3
    gap = jnp.abs(key_tile - query_tile)
    reach_row = meta[AT_WIN + 3 * head + 1]
    reach_tile = meta[AT_WIN + 3 * head + 2]
    inner = jnp.where(reach_row > 0, reach_tile, -1)
    first = jnp.where(meta[AT_ROW_LO] > 0, inner, -1)
    last = jnp.where(meta[AT_ROW_HI] > 0, inner, -1)
    out = []
    for low, high in ((first, inner), (inner, inner), (inner, last)):
        limit = jnp.where(line == 0, low, jnp.where(line == 2, high, reach_tile))
        out.append(jnp.where(gap <= limit, 0.0, NEG).astype(F32))
    return out


def dot_t(q, k):
    return lax.dot_general(q, k, (((1,), (1,)), ((), ())), preferred_element_type=F32)


def lines_of(i):
    return slice(i * W, (i + 3) * W)


def softmax_parts(scores):
    top = functools.reduce(jnp.maximum, [jnp.max(s, axis=-1, keepdims=True) for s in scores])
    return [jnp.exp2((s - top) * SCALE2).astype(BF16) for s in scores], top


def closing(mixed, top):
    total = mixed[:, HD:]
    return (mixed[:, :HD] / total).astype(BF16), top * SCALE2 + jnp.log(total) * LOG2E


def remote_kernel(start, group, steps, meta, *refs):
    ob, oa = refs[3 * group + 5 : 3 * group + 7]
    sb, sa = refs[-2:]
    step = pl.program_id(0)

    @pl.when(step < steps)
    def _():
        remote_step(start, group, step, meta, *refs)

    @pl.when(step == steps)
    def _():
        ob[0] = sb[...].astype(BF16)
        oa[0] = sa[...].astype(BF16)


def remote_step(start, group, step, meta, *refs):
    qb, qa, inverse = refs[:3]
    refs = refs[3:]
    ks, vs, gains = refs[:group], refs[group : 2 * group], refs[2 * group : 3 * group]
    low, high, ob, oa = refs[3 * group : 3 * group + 4]
    kxs, vxs = refs[3 * group + 4 : 4 * group + 4], refs[4 * group + 4 : 5 * group + 4]
    sb, sa = refs[-2:]

    @pl.when(step == 0)
    def _():
        sb[...] = jnp.zeros_like(sb)
        sa[...] = jnp.zeros_like(sa)
        fill_ones(vxs)

    for g in range(group):
        fill_lines(kxs[g], vxs[g], ks[g], vs[g], inverse, gains[g], low.at[pl.ds(g, 1)], high.at[pl.ds(g, 1)])
    scores = []
    for g in range(group):
        head = meta[AT_P + start + step * group + g]
        masks = biases(meta, head)
        parts = [
            dot_t(q[g, i * W : (i + 1) * W], kxs[g][j, lines_of(i)]) + masks[i]
            for j, q in ((0, qb), (1, qa))
            for i in range(3)
        ]
        scores.append(jnp.concatenate(parts, axis=0))
    lane = lax.broadcasted_iota(jnp.int32, (3 * W, HD), 1)
    for g in range(group):
        (weights,), top = softmax_parts([scores[g]])
        mixed = jnp.concatenate(
            [
                jnp.dot(
                    weights[(3 * j + i) * W : (3 * j + i + 1) * W],
                    vxs[g][j, lines_of(i)],
                    preferred_element_type=F32,
                )
                for j in range(2)
                for i in range(3)
            ],
            axis=0,
        )
        mixed, lse = closing(mixed, top)
        ob[g] = mixed[: 3 * W]
        oa[g] = mixed[3 * W :]
        for j, st in ((0, sb), (1, sa)):
            full = lse[3 * W * j : 3 * W * (j + 1)]
            piece = full.astype(BF16).astype(F32)
            rest = full - piece
            middle = rest.astype(BF16).astype(F32)
            both = jnp.where(lane < 32, piece, jnp.where(lane < 64, middle, rest - middle))
            both = jnp.where(lane < 96, both, 0.0)
            st[...] = jnp.where((lane & 31) == step * group + g, both, st[...])


def remote_partial(meta, qb, qa, k, v, gain, inverse, low, high, start, count):
    group = 2
    rows = low.shape[0]
    steps = count // group
    last = min(rows // group, steps) - 1

    def at(j):
        return lambda s, meta: (0, 0, 0, meta[AT_P + start + jnp.minimum(s, steps - 1) * group + j])

    heads = [pl.BlockSpec((2, 3, W, HD), at(j)) for j in range(group)]
    gains = [pl.BlockSpec((1, HD), lambda s, meta, at=at(j): at(s, meta)[2:]) for j in range(group)]
    q_spec = pl.BlockSpec(
        (group, 3 * W, HD), lambda s, meta: (start // group + jnp.minimum(s, steps - 1), 0, 0)
    )
    o_spec = pl.BlockSpec((group, 3 * W, HD), lambda s, meta: (s, 0, 0))
    row_spec = pl.BlockSpec((group, 2, 2, W, HD), lambda s, meta: (jnp.minimum(s, last), 0, 0, 0, 0))
    out = jax.ShapeDtypeStruct((count + 1, 3 * W, HD), BF16)
    return pl.pallas_call(
        functools.partial(remote_kernel, start, group, steps),
        grid_spec=pltpu.PrefetchScalarGridSpec(
            num_scalar_prefetch=1,
            grid=(steps + 1,),
            in_specs=[q_spec, q_spec, whole((2, 3, W, HD))]
            + heads * 2
            + gains
            + [row_spec, row_spec],
            out_specs=[o_spec, o_spec],
            scratch_shapes=line_scratch(group) + [pltpu.VMEM((3 * W, HD), F32)] * 2,
        ),
        out_shape=[out, out],
        compiler_params=params(),
        cost_estimate=estimate(count, 480 * 240),
        name="remote_partial",
    )(meta, qb, qa, inverse, *([k] * group), *([v] * group), *([gain] * group), low, high)


def own_kernel(group, split, meta, *refs):
    qinverse, kinverse = refs[:2]
    refs = refs[2:]
    qs, ks, vs, qgains, kgains = (refs[group * n : group * (n + 1)] for n in range(5))
    refs = refs[5 * group :]
    chunks = 1 if split is None else 2
    lows, highs = (refs[group * chunks * n : group * chunks * (n + 1)] for n in range(2))
    out, lse_out = refs[2 * group * chunks : 2 * group * chunks + 2]
    refs = refs[2 * group * chunks + 2 :]
    kxs, vxs = refs[:group], refs[group:]
    step = pl.program_id(0)
    start = 0

    @pl.when(step == 0)
    def _():
        lse_out[...] = jnp.zeros_like(lse_out)
        fill_ones(vxs)

    def line_of(blocks, g):
        if split is None:
            return blocks[g]
        early = meta[AT_PLACE + start + step * group + g] < split
        return jnp.where(early, blocks[g][...], blocks[group + g][...])

    for g in range(group):
        fill_lines(
            kxs[g], vxs[g], ks[g], vs[g], kinverse, kgains[g], line_of(lows, g), line_of(highs, g)
        )
    scores = []
    for g in range(group):
        head = meta[AT_P + start + step * group + g]
        masks = biases(meta, head)
        cross = jnp.where(meta[AT_WIN + 3 * head] > 0, 0.0, NEG)
        both = ([], [])
        qn = normed(qs[g][...], qinverse[...], qgains[g][...].reshape(1, 1, 1, HD))
        for i in range(3):
            qi = qn[:, i].reshape(2 * W, HD)
            far = masks[i] + cross
            for j in range(2):
                mask = jnp.concatenate([masks[i], far] if j == 0 else [far, masks[i]], axis=0)
                both[j].append(dot_t(qi, kxs[g][j, lines_of(i)]) + mask)
        scores.append([jnp.concatenate(part, axis=0) for part in both])
    lane = lax.broadcasted_iota(jnp.int32, (2 * W, HD), 1)
    for g in range(group):
        weights, top = softmax_parts(scores[g])
        for i in range(3):
            at = slice(2 * W * i, 2 * W * (i + 1))
            mixed = sum(
                jnp.dot(weights[j][at], vxs[g][j, lines_of(i)], preferred_element_type=F32) for j in range(2)
            )
            mixed, lse = closing(mixed, top[at])
            out[g, :, i] = mixed.reshape(2, W, HD)
            old = lse_out[:, i].reshape(2 * W, HD)
            lse_out[:, i] = jnp.where(lane == start + step * group + g, lse, old).reshape(2, W, HD)


def own_partial(meta, q, k, v, qgain, kgain, qinverse, kinverse, lows, highs, split, count):
    group = 2
    start = 0
    heads = [head_spec(AT_P, start, group, j) for j in range(group)]
    gains = [gain_spec(AT_P, start, group, j) for j in range(group)]

    def row_spec(first, rows, j):
        def at(s, meta):
            place = meta[AT_PLACE + start + s * group + j] - first
            return (jnp.clip(place, 0, rows - 1), 0, 0, 0, 0)

        return pl.BlockSpec((1, 2, 2, W, HD), at)

    rows = [
        row_spec(first, chunk.shape[0], j)
        for first, chunk in zip((0, split), lows)
        for j in range(group)
    ]
    return pl.pallas_call(
        functools.partial(own_kernel, group, split),
        grid_spec=pltpu.PrefetchScalarGridSpec(
            num_scalar_prefetch=1,
            grid=(count // group,),
            in_specs=[whole((2, 3, W, HD))] * 2 + heads * 3 + gains * 2 + rows * 2,
            out_specs=[
                pl.BlockSpec((group, 2, 3, W, HD), lambda s, meta: (s, 0, 0, 0, 0)),
                whole((2, 3, W, HD)),
            ],
            scratch_shapes=line_scratch(group),
        ),
        out_shape=[
            jax.ShapeDtypeStruct((count, 2, 3, W, HD), BF16),
            jax.ShapeDtypeStruct((2, 3, W, HD), F32),
        ],
        compiler_params=params(),
        cost_estimate=estimate(count, 480 * 480),
        name="own_partial",
    )(
        meta,
        qinverse,
        kinverse,
        *([q] * group),
        *([k] * group),
        *([v] * group),
        *([qgain] * group),
        *([kgain] * group),
        *[chunk for chunk in lows for _ in range(group)],
        *[chunk for chunk in highs for _ in range(group)],
    )


def merge_kernel(group, starts, meta, part, lse, ob, oa, sb, sa, *refs):
    out, buffer, sems = refs[-3:]
    step = pl.program_id(0)
    steps = pl.num_programs(0)
    slot = slot_at(step, group, starts)
    at = lax.rem(step, 2)

    def copy(step, buffer_at, g):
        head = meta[AT_P + slot_at(step, group, starts) + g]
        return pltpu.make_async_copy(
            buffer.at[buffer_at, g],
            out.at[:, :, :, pl.ds(pl.multiple_of(head * HD, HD), HD)],
            sems.at[buffer_at, g],
        )

    @pl.when(step >= 2)
    def _():
        for g in range(group):
            copy(step - 2, at, g).wait()

    lane = lax.broadcasted_iota(jnp.int32, (3 * W, HD), 1)
    for g in range(group):
        merged = slot + g < meta[AT_NF]
        for j, o, st, flag in ((0, ob, sb, AT_FRAME_LO), (1, oa, sa, AT_FRAME_HI)):
            mine = jnp.where(lane == slot + g, lse[j].reshape(3 * W, HD), 0.0)
            own = jnp.sum(mine, axis=1, keepdims=True)
            pieces = jnp.where(((lane & 31) == step * group + g) & (lane < 96), st[0].astype(F32), 0.0)
            other = jnp.sum(pieces, axis=1, keepdims=True)
            use = merged & (meta[flag] > 0)
            other = jnp.where(use, other, NEG)
            top = jnp.maximum(own, other)
            own_weight = jnp.exp2(own - top)
            other_weight = jnp.exp2(other - top)
            scale = 1.0 / (own_weight + other_weight)
            far = jnp.where(use, o[g].astype(F32), 0.0)
            mixed = part[g, j].reshape(3 * W, HD).astype(F32) * (own_weight * scale)
            mixed = mixed + far * (other_weight * scale)
            buffer[at, g, j] = mixed.astype(BF16).reshape(3, W, HD)
    for g in range(group):
        copy(step, at, g).start()

    @pl.when(step == steps - 1)
    def _():
        for g in range(group):
            if starts[2] > 1:
                copy(step - 1, 1 - at, g).wait()
            copy(step, at, g).wait()


def slot_at(step, group, starts):
    base, tail, _, turn = starts
    return jnp.where(step < turn, base + step * group, tail + (step - turn) * group)


def merge(meta, out, part, lse, o_below, o_above, base, tail, chunk):
    group = 2
    turn = chunk // group
    steps = turn + (0 if tail is None else (NH - tail) // group)
    starts = (base, NH if tail is None else tail, steps, turn)
    stop = o_below.shape[0] - 1
    o_spec = pl.BlockSpec((group, 3 * W, HD), lambda s, meta: (jnp.minimum(s, turn - 1), 0, 0))
    stat_spec = pl.BlockSpec((1, 3 * W, HD), lambda s, meta: (stop, 0, 0))
    return pl.pallas_call(
        functools.partial(merge_kernel, group, starts),
        grid_spec=pltpu.PrefetchScalarGridSpec(
            num_scalar_prefetch=1,
            grid=(steps,),
            in_specs=[
                pl.BlockSpec(
                    (group, 2, 3, W, HD), lambda s, meta: (slot_at(s, group, starts) // group, 0, 0, 0, 0)
                ),
                whole((2, 3, W, HD)),
                o_spec,
                o_spec,
                stat_spec,
                stat_spec,
            ]
            + ([] if out is None else [pl.BlockSpec(memory_space=pl.ANY)]),
            out_specs=pl.BlockSpec(memory_space=pl.ANY),
            scratch_shapes=[
                pltpu.VMEM((2, group, 2, 3, W, HD), BF16),
                pltpu.SemaphoreType.DMA((2, group)),
            ],
        ),
        out_shape=jax.ShapeDtypeStruct((2, 3, W, NH * HD), BF16),
        input_output_aliases={} if out is None else {7: 0},
        compiler_params=params(),
        cost_estimate=pl.CostEstimate(flops=steps * 2_000_000, bytes_accessed=steps * 800_000, transcendentals=0),
        name="merge",
    )(meta, part, lse, o_below, o_above, o_below, o_above, *([] if out is None else [out]))


def order_of(keys):
    ids = jnp.arange(NH, dtype=jnp.int32)
    unique = keys * NH + ids
    rank = jnp.sum((unique[None, :] < unique[:, None]).astype(jnp.int32), axis=1)
    return jnp.sum(jnp.where(rank[:, None] == ids[None, :], ids[:, None], 0), axis=0), rank


def shifts(axis):
    count = lax.axis_size(axis)
    forward = [(i, i + 1) for i in range(count - 1)]
    return forward, [(b, a) for a, b in forward]


def attention(frame_slots, row_slots, first, meta, q, k, v, q_gain, k_gain, q_inverse, k_inverse):
    up_frame, down_frame = shifts("frame")
    up_row, down_row = shifts("height")
    q_up, q_down = pack_queries(meta, q, q_gain, q_inverse, frame_slots)
    qb = lax.ppermute(q_up, "frame", up_frame)
    qa = lax.ppermute(q_down, "frame", down_frame)
    lows, highs = [], []
    for start, count in ((0, first), (first, row_slots - first)):
        up, down = pack_rows(meta, k, v, k_gain, k_inverse, start, count)
        lows.append(lax.ppermute(up, "height", up_row))
        highs.append(lax.ppermute(down, "height", down_row))
    remote = []
    for part, (start, count) in enumerate(((0, first), (first, frame_slots - first))):
        ob, oa = remote_partial(
            meta, qb, qa, k, v, k_gain, k_inverse, lows[part], highs[part], start, count
        )
        remote.append((lax.ppermute(oa, "frame", up_frame), lax.ppermute(ob, "frame", down_frame)))
    part, lse = own_partial(
        meta, q, k, v, q_gain, k_gain, q_inverse, k_inverse, lows, highs, first, NH
    )
    out = merge(meta, None, part, lse, *remote[0], 0, frame_slots, first)
    return merge(meta, out, part, lse, *remote[1], first, None, frame_slots - first)


def squares_of(raw):
    values = raw.astype(F32)
    return jnp.sum(values * values, axis=-1)


def body(q, k, v, q_gain, k_gain, window):
    width_total = q.shape[3] * lax.axis_size("head")
    query_sum, key_sum = lax.psum((squares_of(q), squares_of(k)), "head")

    def inverse_of(total):
        return jnp.broadcast_to(lax.rsqrt(total / width_total + EPS)[..., None], (2, 3, W, HD))

    frame_reach, row_reach = window[:, 0], window[:, 1]
    frame_at, row_at = lax.axis_index("frame"), lax.axis_index("height")
    flags = jnp.stack(
        [
            row_at > 0,
            row_at < lax.axis_size("height") - 1,
            frame_at > 0,
            frame_at < lax.axis_size("frame") - 1,
        ]
    ).astype(jnp.int32)
    frame_list, frame_rank = order_of((1 - frame_reach) * 2 + (1 - row_reach))
    row_list, row_rank = order_of((1 - row_reach) * 2 + (1 - frame_reach))
    ids = jnp.arange(NH, dtype=jnp.int32)
    place = jnp.sum(jnp.where(frame_rank[:, None] == ids[None, :], row_rank[:, None], 0), axis=0)
    meta = jnp.concatenate(
        [
            frame_list,
            row_list,
            place,
            window.reshape(-1),
            flags,
            jnp.sum(frame_reach, keepdims=True),
        ]
    ).astype(jnp.int32)
    return attention(
        NH,
        NH,
        8,
        meta,
        q,
        k,
        v,
        q_gain[None],
        k_gain[None],
        inverse_of(query_sum),
        inverse_of(key_sum),
    )


def solution(mesh):
    placed = (
        P("frame", "height", None, "head"),
        P("frame", "height", None, "head"),
        P("frame", "height", None, "head"),
        P("head"),
        P("head"),
        P("head", None),
    )
    return jax.shard_map(
        body,
        mesh=mesh,
        in_specs=placed,
        out_specs=P("frame", "height", None, "head"),
        check_vma=False,
    )
```

```python
import functools
import math

import jax
import jax.numpy as jnp
from jax import lax
from jax.experimental import pallas as pl
from jax.experimental.pallas import tpu as pltpu
from jax.sharding import PartitionSpec as P

HD = 128
W = 80
NH = 20
FIRST = 12
EPS = 1e-06
NEG = -1e30
FAR = 100
LOG2E = math.log2(math.e)
SCALE2 = LOG2E / math.sqrt(HD)
F32 = jnp.float32
BF16 = jnp.bfloat16


def params(mib=12):
    return pltpu.CompilerParams(vmem_limit_bytes=mib * 1024 * 1024)


def cost(microseconds):
    return pl.CostEstimate(flops=0, bytes_accessed=int(microseconds * 3_000_000), transcendentals=0)


def normed(raw, inverse, gain):
    return (raw.astype(F32) * inverse * gain).astype(BF16)


def lanes(g):
    return slice(g * HD, (g + 1) * HD)


def heads_spec(start, group):
    return pl.BlockSpec((2, 3, W, group * HD), lambda s, window: (0, 0, 0, start // group + s))


def gains_spec(start, group):
    return pl.BlockSpec((1, group * HD), lambda s, window: (0, start // group + s))


def whole(shape):
    return pl.BlockSpec(shape, lambda s, window: (0,) * len(shape))


def pack_queries_kernel(group, window, raw, gain, inverse, up, down):
    for g in range(group):
        q = normed(raw[:, :, :, lanes(g)], inverse[...], gain[:, lanes(g)].reshape(1, 1, 1, HD))
        up[g] = q[1].reshape(3 * W, HD)
        down[g] = q[0].reshape(3 * W, HD)


def pack_rows_kernel(group, window, keys, values, gain, inverse, up, down):
    for g in range(group):
        k_gain = gain[:, lanes(g)].reshape(1, 1, HD)
        for out, row in ((up, 2), (down, 0)):
            out[g, 0] = normed(keys[:, row, :, lanes(g)], inverse[:, row], k_gain)
            out[g, 1] = values[:, row, :, lanes(g)]


def group_of(start, count):
    return max(n for n in (1, 2, 4, 5) if count % n == 0 and start % n == 0)


def pack_queries(window, q, gain, inverse, start, count):
    group = group_of(start, count)
    out = jax.ShapeDtypeStruct((count, 3 * W, HD), BF16)
    out_spec = pl.BlockSpec((group, 3 * W, HD), lambda s, window: (s, 0, 0))
    return pl.pallas_call(
        functools.partial(pack_queries_kernel, group),
        grid_spec=pltpu.PrefetchScalarGridSpec(
            num_scalar_prefetch=1,
            grid=(count // group,),
            in_specs=[heads_spec(start, group), gains_spec(start, group), whole((2, 3, W, HD))],
            out_specs=[out_spec, out_spec],
        ),
        out_shape=[out, out],
        compiler_params=params(),
        cost_estimate=cost(0.1 * count),
        name="pack_queries",
    )(window, q, gain, inverse)


def pack_rows(window, k, v, gain, inverse, start, count):
    group = group_of(start, count)
    out = jax.ShapeDtypeStruct((count, 2, 2, W, HD), BF16)
    out_spec = pl.BlockSpec((group, 2, 2, W, HD), lambda s, window: (s, 0, 0, 0, 0))
    return pl.pallas_call(
        functools.partial(pack_rows_kernel, group),
        grid_spec=pltpu.PrefetchScalarGridSpec(
            num_scalar_prefetch=1,
            grid=(count // group,),
            in_specs=[heads_spec(start, group)] * 2 + [gains_spec(start, group), whole((2, 3, W, HD))],
            out_specs=[out_spec, out_spec],
        ),
        out_shape=[out, out],
        compiler_params=params(),
        cost_estimate=cost(0.15 * count),
        name="pack_rows",
    )(window, k, v, gain, inverse)


def fill_lines(kx, vx, k, v, inverse, gain, low, high):
    kn = normed(k, inverse, gain.reshape(1, 1, 1, HD))
    for j in range(2):
        kx[j, 0:W] = low[0, j]
        kx[j, W : 4 * W] = kn[j].reshape(3 * W, HD)
        kx[j, 4 * W : 5 * W] = high[0, j]
        vx[j, 0:W, 0:HD] = low[1, j]
        vx[j, W : 4 * W, 0:HD] = v[j].reshape(3 * W, HD)
        vx[j, 4 * W : 5 * W, 0:HD] = high[1, j]


def line_scratch(group):
    return [pltpu.VMEM((2, 5 * W, HD), BF16)] * group + [pltpu.VMEM((2, 5 * W, 2 * HD), BF16)] * group


def inside(axis):
    at = lax.axis_index(axis)
    return at > 0, at < lax.axis_size(axis) - 1


def fill_ones(values):
    for vx in values:
        vx[:, :, HD:] = jnp.ones((2, 5 * W, HD), BF16)


def fill_gaps(gaps):
    lane = lax.broadcasted_iota(jnp.int32, (W, 3 * W), 1)
    line = (lane >= W).astype(jnp.int32) + (lane >= 2 * W).astype(jnp.int32)
    key_tile = (lane - W * line) >> 3
    query_tile = lax.broadcasted_iota(jnp.int32, (W, 3 * W), 0) >> 3
    gap = jnp.abs(key_tile - query_tile)
    below, above = inside("height")
    no_low = jnp.where(below, 0, FAR)
    no_high = jnp.where(above, 0, FAR)
    for reach in range(2):
        for i in range(3):
            low = FAR if reach == 0 else (no_low if i == 0 else 0)
            high = FAR if reach == 0 else (no_high if i == 2 else 0)
            gaps[reach, i] = gap + jnp.where(line == 0, low, 0) + jnp.where(line == 2, high, 0)


def biases(gaps, window, head):
    reach_row, reach_tile = jnp.minimum(window[head, 1], 1), window[head, 2]
    return [jnp.where(gaps[reach_row, i] <= reach_tile, 0.0, NEG).astype(F32) for i in range(3)]


def dot_t(q, k):
    return lax.dot_general(q, k, (((1,), (1,)), ((), ())), preferred_element_type=F32)


def lines_of(i):
    return slice(i * W, (i + 3) * W)


def row_max(s):
    return jnp.max(s, axis=-1, keepdims=True)


def weights_of(s, top):
    return jnp.exp2((s - top) * SCALE2).astype(BF16)


def divided(mixed):
    total = mixed[:, HD:]
    inverse = pl.reciprocal(total, approx=True)
    inverse = inverse * (2.0 - total * inverse)
    return (mixed[:, :HD] * inverse).astype(BF16)


def mark(st, at, here, top, mixed):
    st[0, at] = jnp.where(here, top, st[0, at])
    st[1, at] = jnp.where(here, mixed[:, HD:], st[1, at])


def lse_of(st):
    return st[0] * SCALE2 + jnp.log(st[1]) * LOG2E


def pieces_of(full, lane):
    high = full.astype(BF16).astype(F32)
    rest = full - high
    middle = rest.astype(BF16).astype(F32)
    low = rest - middle
    return jnp.where(lane < 32, high, jnp.where(lane < 64, middle, jnp.where(lane < 96, low, 0.0))).astype(BF16)


def both_kernel(start, group, steps, window, *refs):
    st_own, st_far = refs[-2:]
    ob, oa, own_stats = refs[-6 - 2 * group : -3 - 2 * group]
    step = pl.program_id(0)

    @pl.when(step < steps)
    def _():
        both_step(start, group, step, window, *refs)

    @pl.when(step == steps)
    def _():
        lane = lax.broadcasted_iota(jnp.int32, (3 * W, HD), 1)
        for j in range(2):
            own_stats[j] = lse_of(st_own[j])
        ob[0] = pieces_of(lse_of(st_far[0]), lane)
        oa[0] = pieces_of(lse_of(st_far[1]), lane)


def both_step(start, group, step, window, *refs):
    qinverse, kinverse, qb, qa, q, k, v, qgain, kgain, low, high, part, ob, oa, _ = refs[:15]
    kxs, vxs = refs[15 : 15 + group], refs[15 + group : 15 + 2 * group]
    gaps, st_own, st_far = refs[-3:]
    slot = start + step * group

    @pl.when(step == 0)
    def _():
        for st in (st_own, st_far):
            for j in range(2):
                st[j, 0] = jnp.zeros((3 * W, HD), F32)
                st[j, 1] = jnp.ones((3 * W, HD), F32)
        fill_ones(vxs)
        fill_gaps(gaps)

    scores = []
    for g in range(group):
        own_keys, own_values = k[:, :, :, lanes(g)], v[:, :, :, lanes(g)]
        fill_lines(kxs[g], vxs[g], own_keys, own_values, kinverse[...], kgain[:, lanes(g)], low[g], high[g])
        masks = biases(gaps, window, slot + g)
        cross = jnp.where(window[slot + g, 0] > 0, 0.0, NEG)
        qn = normed(q[:, :, :, lanes(g)], qinverse[...], qgain[:, lanes(g)].reshape(1, 1, 1, HD))
        for i in range(3):
            own = qn[:, i].reshape(2 * W, HD)
            far = masks[i] + cross
            for j, far_q in ((0, qb), (1, qa)):
                queries = jnp.concatenate([own, far_q[g, i * W : (i + 1) * W]], axis=0)
                order = [masks[i], far, masks[i]] if j == 0 else [far, masks[i], masks[i]]
                raw = dot_t(queries, kxs[g][j, lines_of(i)])
                scores.append([raw[W * n : W * (n + 1)] + order[n] for n in range(3)])
    tops, weights = [], []
    for s0, s1 in zip(scores[::2], scores[1::2]):
        first, second = (row_max(jnp.maximum(s0[n], s1[n])) for n in range(2))
        below, above = row_max(s0[2]), row_max(s1[2])
        tops.append((jnp.concatenate([first, second], axis=0), below, above))
        for s, last in ((s0, below), (s1, above)):
            parts = [weights_of(a, b) for a, b in zip(s, (first, second, last))]
            weights.append(jnp.concatenate(parts, axis=0))
    lane = lax.broadcasted_iota(jnp.int32, (W, HD), 1)
    for g in range(group):
        here = (lane & 31) == step * group + g
        for i in range(3):
            w0, w1 = weights[6 * g + 2 * i : 6 * g + 2 * i + 2]
            top, top_b, top_a = tops[3 * g + i]
            m0 = jnp.dot(w0, vxs[g][0, lines_of(i)], preferred_element_type=F32)
            m1 = jnp.dot(w1, vxs[g][1, lines_of(i)], preferred_element_type=F32)
            at = slice(i * W, (i + 1) * W)
            for n in range(2):
                own = m0[W * n : W * (n + 1)] + m1[W * n : W * (n + 1)]
                part[g, n, i] = divided(own)
                mark(st_own.at[n], at, here, top[W * n : W * (n + 1)], own)
            for n, o, far, far_top in ((0, ob, m0[2 * W :], top_b), (1, oa, m1[2 * W :], top_a)):
                o[g, at] = divided(far)
                mark(st_far.at[n], at, here, far_top, far)


def both_partial(window, qb, qa, q, k, v, qgain, kgain, qinverse, kinverse, low, high, start, count):
    group = 2
    steps = count // group

    def step_of(s):
        return jnp.minimum(s, steps - 1)

    heads = pl.BlockSpec((2, 3, W, group * HD), lambda s, window: (0, 0, 0, start // group + step_of(s)))
    gains = pl.BlockSpec((1, group * HD), lambda s, window: (0, start // group + step_of(s)))
    rows = pl.BlockSpec((group, 2, 2, W, HD), lambda s, window: (step_of(s), 0, 0, 0, 0))
    q_spec = pl.BlockSpec((group, 3 * W, HD), lambda s, window: (step_of(s), 0, 0))
    o_spec = pl.BlockSpec((group, 3 * W, HD), lambda s, window: (s, 0, 0))
    out = jax.ShapeDtypeStruct((count + 1, 3 * W, HD), BF16)
    stat = pltpu.VMEM((2, 2, 3 * W, HD), F32)
    return pl.pallas_call(
        functools.partial(both_kernel, start, group, steps),
        grid_spec=pltpu.PrefetchScalarGridSpec(
            num_scalar_prefetch=1,
            grid=(steps + 1,),
            in_specs=[whole((2, 3, W, HD))] * 2 + [q_spec] * 2 + [heads] * 3 + [gains] * 2 + [rows] * 2,
            out_specs=[
                pl.BlockSpec((group, 2, 3, W, HD), lambda s, window: (step_of(s), 0, 0, 0, 0)),
                o_spec,
                o_spec,
                whole((2, 3 * W, HD)),
            ],
            scratch_shapes=line_scratch(group) + [pltpu.VMEM((2, 3, W, 3 * W), jnp.int32), stat, stat],
        ),
        out_shape=[
            jax.ShapeDtypeStruct((count, 2, 3, W, HD), BF16),
            out,
            out,
            jax.ShapeDtypeStruct((2, 3 * W, HD), F32),
        ],
        compiler_params=params(16),
        cost_estimate=cost(1.1 * count),
        name="both_partial",
    )(window, qinverse, kinverse, qb, qa, q, k, v, qgain, kgain, low, high)


def merge_kernel(start, group, window, part, lse, ob, oa, sb, sa, *refs):
    out, shares = refs[-2:]
    lane = lax.broadcasted_iota(jnp.int32, (3 * W, HD), 1)
    neighbours = inside("frame")
    step = pl.program_id(0)

    @pl.when(step == 0)
    def _():
        for j, st in ((0, sb), (1, sa)):
            pieces = st[0].astype(F32)
            other = pieces + pltpu.roll(pieces, HD - 32, 1) + pltpu.roll(pieces, HD - 64, 1)
            other = jnp.where(neighbours[j], other, NEG)
            own = lse[j]
            top = jnp.maximum(own, other)
            own_weight = jnp.exp2(own - top)
            other_weight = jnp.exp2(other - top)
            scale = 1.0 / (own_weight + other_weight)
            shares[j, 0] = own_weight * scale
            shares[j, 1] = other_weight * scale

    for g in range(group):
        here = lane == step * group + g
        for j, o in ((0, ob), (1, oa)):
            use = (window[start + step * group + g, 0] > 0) & neighbours[j]
            own = jnp.sum(jnp.where(here, shares[j, 0], 0.0), axis=1, keepdims=True)
            other = jnp.sum(jnp.where(here, shares[j, 1], 0.0), axis=1, keepdims=True)
            own = jnp.where(use, own, 1.0)
            other = jnp.where(use, other, 0.0)
            far = jnp.where(use, o[g].astype(F32), 0.0)
            mixed = part[g, j].reshape(3 * W, HD).astype(F32) * own + far * other
            out[j, :, :, lanes(g)] = mixed.astype(BF16).reshape(3, W, HD)


def merge(window, out, part, lse, o_below, o_above, start, count):
    group = group_of(start, count)
    o_spec = pl.BlockSpec((group, 3 * W, HD), lambda s, window: (s, 0, 0))
    stat_spec = pl.BlockSpec((1, 3 * W, HD), lambda s, window: (count, 0, 0))
    return pl.pallas_call(
        functools.partial(merge_kernel, start, group),
        grid_spec=pltpu.PrefetchScalarGridSpec(
            num_scalar_prefetch=1,
            grid=(count // group,),
            in_specs=[
                pl.BlockSpec((group, 2, 3, W, HD), lambda s, window: (s, 0, 0, 0, 0)),
                whole((2, 3 * W, HD)),
                o_spec,
                o_spec,
                stat_spec,
                stat_spec,
            ]
            + ([] if out is None else [pl.BlockSpec(memory_space=pl.ANY)]),
            out_specs=heads_spec(start, group),
            scratch_shapes=[pltpu.VMEM((2, 2, 3 * W, HD), F32)],
        ),
        out_shape=jax.ShapeDtypeStruct((2, 3, W, NH * HD), BF16),
        input_output_aliases={} if out is None else {7: 0},
        compiler_params=params(),
        cost_estimate=cost(0.25 * count),
        name="merge",
    )(window, part, lse, o_below, o_above, o_below, o_above, *([] if out is None else [out]))


def shifts(axis):
    count = lax.axis_size(axis)
    forward = [(i, i + 1) for i in range(count - 1)]
    return forward, [(b, a) for a, b in forward]


def attention(window, q, k, v, q_gain, k_gain, q_inverse, k_inverse):
    up_frame, down_frame = shifts("frame")
    up_row, down_row = shifts("height")
    norms = (q_gain, k_gain, q_inverse, k_inverse)
    chunks = ((0, FIRST), (FIRST, NH - FIRST))
    queries, rows = [], []
    for start, count in chunks:
        rows_up, rows_down = pack_rows(window, k, v, k_gain, k_inverse, start, count)
        rows.append((lax.ppermute(rows_up, "height", up_row), lax.ppermute(rows_down, "height", down_row)))
        q, rows_up, rows_down = lax.optimization_barrier((q, rows_up, rows_down))
        q_up, q_down = pack_queries(window, q, q_gain, q_inverse, start, count)
        queries.append((lax.ppermute(q_up, "frame", up_frame), lax.ppermute(q_down, "frame", down_frame)))
        k, q_up, q_down = lax.optimization_barrier((k, q_up, q_down))
    parts = []
    for n, (start, count) in enumerate(chunks):
        part, ob, oa, lse = both_partial(window, *queries[n], q, k, v, *norms, *rows[n], start, count)
        below, above = lax.ppermute(oa, "frame", up_frame), lax.ppermute(ob, "frame", down_frame)
        parts.append((part, lse, below, above, start, count))
    out = None
    for part in parts:
        out = merge(window, out, *part)
    return out


def squares_of(raw):
    values = raw.astype(F32)
    return jnp.sum(values * values, axis=-1)


def body(q, k, v, q_gain, k_gain, window):
    width_total = q.shape[3] * lax.axis_size("head")
    query_sum, key_sum = lax.psum((squares_of(q), squares_of(k)), "head")

    def inverse_of(total):
        return jnp.broadcast_to(lax.rsqrt(total / width_total + EPS)[..., None], (2, 3, W, HD))

    return attention(
        window, q, k, v, q_gain[None], k_gain[None], inverse_of(query_sum), inverse_of(key_sum)
    )


def solution(mesh):
    placed = (
        P("frame", "height", None, "head"),
        P("frame", "height", None, "head"),
        P("frame", "height", None, "head"),
        P("head"),
        P("head"),
        P("head", None),
    )
    return jax.shard_map(
        body,
        mesh=mesh,
        in_specs=placed,
        out_specs=P("frame", "height", None, "head"),
        check_vma=False,
    )
```

```python
import functools
import math

import jax
import jax.numpy as jnp
from jax import lax
from jax.experimental import pallas as pl
from jax.experimental.pallas import tpu as pltpu
from jax.sharding import PartitionSpec as P

HD = 128
W = 80
NH = 20
FIRST = 10
EPS = 1e-06
NEG = -1e30
FAR = 100
LOG2E = math.log2(math.e)
SCALE2 = LOG2E / math.sqrt(HD)
F32 = jnp.float32
BF16 = jnp.bfloat16


def params(mib=12):
    return pltpu.CompilerParams(vmem_limit_bytes=mib * 1024 * 1024)


def cost(microseconds):
    return pl.CostEstimate(flops=0, bytes_accessed=int(microseconds * 3_000_000), transcendentals=0)


def normed(raw, inverse, gain):
    return (raw.astype(F32) * inverse * gain).astype(BF16)


def lanes(g):
    return slice(g * HD, (g + 1) * HD)


def heads_spec(start, group):
    return pl.BlockSpec((2, 3, W, group * HD), lambda s, window: (0, 0, 0, start // group + s))


def gains_spec(start, group):
    return pl.BlockSpec((1, group * HD), lambda s, window: (0, start // group + s))


def whole(shape):
    return pl.BlockSpec(shape, lambda s, window: (0,) * len(shape))


def pack_queries_kernel(group, window, raw, gain, inverse, first, second):
    for g in range(group):
        q = normed(raw[:, :, :, lanes(g)], inverse[...], gain[:, lanes(g)].reshape(1, 1, 1, HD))
        first[g], second[g] = sides("frame", q[0].reshape(3 * W, HD), q[1].reshape(3 * W, HD))


def pack_rows_kernel(group, window, keys, values, gain, inverse, first, second):
    for g in range(group):
        k_gain = gain[:, lanes(g)].reshape(1, 1, HD)
        for n, row_of in (
            (0, lambda row: normed(keys[:, row, :, lanes(g)], inverse[:, row], k_gain)),
            (1, lambda row: values[:, row, :, lanes(g)]),
        ):
            first[g, n], second[g, n] = sides("height", row_of(0), row_of(2))


def group_of(start, count):
    return max(n for n in (1, 2, 4, 5) if count % n == 0 and start % n == 0)


def pack_queries(window, q, gain, inverse, start, count):
    group = group_of(start, count)
    out = jax.ShapeDtypeStruct((count, 3 * W, HD), BF16)
    out_spec = pl.BlockSpec((group, 3 * W, HD), lambda s, window: (s, 0, 0))
    return pl.pallas_call(
        functools.partial(pack_queries_kernel, group),
        grid_spec=pltpu.PrefetchScalarGridSpec(
            num_scalar_prefetch=1,
            grid=(count // group,),
            in_specs=[heads_spec(start, group), gains_spec(start, group), whole((2, 3, W, HD))],
            out_specs=[out_spec, out_spec],
        ),
        out_shape=[out, out],
        compiler_params=params(),
        cost_estimate=cost(0.1 * count),
        name="pack_queries",
    )(window, q, gain, inverse)


def pack_rows(window, k, v, gain, inverse, start, count):
    group = group_of(start, count)
    out = jax.ShapeDtypeStruct((count, 2, 2, W, HD), BF16)
    out_spec = pl.BlockSpec((group, 2, 2, W, HD), lambda s, window: (s, 0, 0, 0, 0))
    return pl.pallas_call(
        functools.partial(pack_rows_kernel, group),
        grid_spec=pltpu.PrefetchScalarGridSpec(
            num_scalar_prefetch=1,
            grid=(count // group,),
            in_specs=[heads_spec(start, group)] * 2 + [gains_spec(start, group), whole((2, 3, W, HD))],
            out_specs=[out_spec, out_spec],
        ),
        out_shape=[out, out],
        compiler_params=params(),
        cost_estimate=cost(0.15 * count),
        name="pack_rows",
    )(window, k, v, gain, inverse)


def fill_lines(kx, vx, k, v, inverse, gain, first, second):
    kn = normed(k, inverse, gain.reshape(1, 1, 1, HD))
    low, high = sides("height", first[...], second[...])
    for j in range(2):
        kx[j, 0:W] = low[0, j]
        kx[j, W : 4 * W] = kn[j].reshape(3 * W, HD)
        kx[j, 4 * W : 5 * W] = high[0, j]
        vx[j, 0:W, 0:HD] = low[1, j]
        vx[j, W : 4 * W, 0:HD] = v[j].reshape(3 * W, HD)
        vx[j, 4 * W : 5 * W, 0:HD] = high[1, j]


def line_scratch(group):
    return [pltpu.VMEM((2, 5 * W, HD), BF16)] * group + [pltpu.VMEM((2, 5 * W, 2 * HD), BF16)] * group


def even(axis):
    return lax.rem(lax.axis_index(axis), 2) == 0


def sides(axis, first, second):
    return jnp.where(even(axis), second, first), jnp.where(even(axis), first, second)


def inside(axis):
    at = lax.axis_index(axis)
    return at > 0, at < lax.axis_size(axis) - 1


def fill_ones(values):
    for vx in values:
        vx[:, :, HD:] = jnp.ones((2, 5 * W, HD), BF16)


def fill_gaps(gaps):
    lane = lax.broadcasted_iota(jnp.int32, (W, 3 * W), 1)
    line = (lane >= W).astype(jnp.int32) + (lane >= 2 * W).astype(jnp.int32)
    key_tile = (lane - W * line) >> 3
    query_tile = lax.broadcasted_iota(jnp.int32, (W, 3 * W), 0) >> 3
    gap = jnp.abs(key_tile - query_tile)
    below, above = inside("height")
    no_low = jnp.where(below, 0, FAR)
    no_high = jnp.where(above, 0, FAR)
    for reach in range(2):
        for i in range(3):
            low = FAR if reach == 0 else (no_low if i == 0 else 0)
            high = FAR if reach == 0 else (no_high if i == 2 else 0)
            gaps[reach, i] = gap + jnp.where(line == 0, low, 0) + jnp.where(line == 2, high, 0)


def biases(gaps, window, head):
    reach_row, reach_tile = jnp.minimum(window[head, 1], 1), window[head, 2]
    return [jnp.where(gaps[reach_row, i] <= reach_tile, 0.0, NEG).astype(F32) for i in range(3)]


def dot_t(q, k):
    return lax.dot_general(q, k, (((1,), (1,)), ((), ())), preferred_element_type=F32)


def lines_of(i):
    return slice(i * W, (i + 3) * W)


def row_max(s):
    return jnp.max(s, axis=-1, keepdims=True)


def weights_of(s, top):
    return jnp.exp2((s - top) * SCALE2).astype(BF16)


def divided(mixed):
    total = mixed[:, HD:]
    inverse = pl.reciprocal(total, approx=True)
    inverse = inverse * (2.0 - total * inverse)
    return (mixed[:, :HD] * inverse).astype(BF16)


def mark(st, at, here, top, mixed):
    st[0, at] = jnp.where(here, top, st[0, at])
    st[1, at] = jnp.where(here, mixed[:, HD:], st[1, at])


def lse_of(st):
    return st[0] * SCALE2 + jnp.log(st[1]) * LOG2E


def pieces_of(full, lane):
    high = full.astype(BF16).astype(F32)
    rest = full - high
    middle = rest.astype(BF16).astype(F32)
    low = rest - middle
    return jnp.where(lane < 32, high, jnp.where(lane < 64, middle, jnp.where(lane < 96, low, 0.0))).astype(BF16)


def partial_kernel(far, start, group, steps, window, kinverse, k, v, kgain, low, high, *refs):
    if far:
        qb, qa, ob, oa = refs[:4]
    else:
        q, qgain, qinverse, part, own_stats = refs[:5]
    kxs, vxs = refs[-2 - 2 * group : -2 - group], refs[-2 - group : -2]
    gaps, st = refs[-2:]
    step = pl.program_id(0)

    @pl.when(step == 0)
    def _():
        for j in range(2):
            st[j, 0] = jnp.zeros((3 * W, HD), F32)
            st[j, 1] = jnp.ones((3 * W, HD), F32)
        fill_ones(vxs)
        fill_gaps(gaps)

    @pl.when(step < steps)
    def _():
        for g in range(group):
            own_keys, own_values = k[:, :, :, lanes(g)], v[:, :, :, lanes(g)]
            fill_lines(
                kxs[g], vxs[g], own_keys, own_values, kinverse[...], kgain[:, lanes(g)], low.at[g], high.at[g]
            )
        if far:
            far_step(start, group, step, window, qb, qa, ob, oa, kxs, vxs, gaps, st)
        else:
            own_step(start, group, step, window, q, qgain, qinverse, part, kxs, vxs, gaps, st)

    if far:

        @pl.when(step == steps)
        def _():
            lane = lax.broadcasted_iota(jnp.int32, (3 * W, HD), 1)
            below, above = (pieces_of(lse_of(st[j]), lane) for j in range(2))
            ob[0], oa[0] = sides("frame", below, above)

    else:

        @pl.when(step == steps - 1)
        def _():
            for j in range(2):
                own_stats[j] = lse_of(st[j])


def marked_lanes(step, group, g):
    return (lax.broadcasted_iota(jnp.int32, (W, HD), 1) & 31) == step * group + g


def far_step(start, group, step, window, qb, qa, ob, oa, kxs, vxs, gaps, st):
    scores = []
    for g in range(group):
        masks = biases(gaps, window, start + step * group + g)
        for i in range(3):
            at = slice(i * W, (i + 1) * W)
            asked = sides("frame", qb[g, at], qa[g, at])
            scores += [dot_t(asked[j], kxs[g][j, lines_of(i)]) + masks[i] for j in range(2)]
    tops = [row_max(s) for s in scores]
    weights = [weights_of(s, top) for s, top in zip(scores, tops)]
    for g in range(group):
        here = marked_lanes(step, group, g)
        for i in range(3):
            at, n = slice(i * W, (i + 1) * W), 6 * g + 2 * i
            mixed = [
                jnp.dot(weights[n + j], vxs[g][j, lines_of(i)], preferred_element_type=F32) for j in range(2)
            ]
            for j in range(2):
                mark(st.at[j], at, here, tops[n + j], mixed[j])
            ob[g, at], oa[g, at] = sides("frame", divided(mixed[0]), divided(mixed[1]))


def own_step(start, group, step, window, q, qgain, qinverse, part, kxs, vxs, gaps, st):
    scores = []
    for g in range(group):
        head = start + step * group + g
        masks = biases(gaps, window, head)
        cross = jnp.where(window[head, 0] > 0, 0.0, NEG)
        qn = normed(q[:, :, :, lanes(g)], qinverse[...], qgain[:, lanes(g)].reshape(1, 1, 1, HD))
        for i in range(3):
            own = qn[:, i].reshape(2 * W, HD)
            other = masks[i] + cross
            for j in range(2):
                raw = dot_t(own, kxs[g][j, lines_of(i)])
                order = (masks[i], other) if j == 0 else (other, masks[i])
                scores.append([raw[W * n : W * (n + 1)] + order[n] for n in range(2)])
    tops, weights = [], []
    for s0, s1 in zip(scores[::2], scores[1::2]):
        top = [row_max(jnp.maximum(s0[n], s1[n])) for n in range(2)]
        tops.append(top)
        for s in (s0, s1):
            weights.append(jnp.concatenate([weights_of(a, b) for a, b in zip(s, top)], axis=0))
    for g in range(group):
        here = marked_lanes(step, group, g)
        for i in range(3):
            at, n = slice(i * W, (i + 1) * W), 3 * g + i
            m0, m1 = (
                jnp.dot(weights[2 * n + j], vxs[g][j, lines_of(i)], preferred_element_type=F32)
                for j in range(2)
            )
            for f in range(2):
                own = m0[W * f : W * (f + 1)] + m1[W * f : W * (f + 1)]
                part[g, f, i] = divided(own)
                mark(st.at[f], at, here, tops[n][f], own)


def partial_call(far, window, k, v, kgain, kinverse, low, high, asked, start, count):
    group = 2
    steps = count // group

    def step_of(s):
        return jnp.minimum(s, steps - 1)

    heads = pl.BlockSpec((2, 3, W, group * HD), lambda s, window: (0, 0, 0, start // group + step_of(s)))
    gains = pl.BlockSpec((1, group * HD), lambda s, window: (0, start // group + step_of(s)))
    rows = pl.BlockSpec((group, 2, 2, W, HD), lambda s, window: (step_of(s), 0, 0, 0, 0))
    norms = whole((2, 3, W, HD))
    if far:
        q_spec = pl.BlockSpec((group, 3 * W, HD), lambda s, window: (step_of(s), 0, 0))
        o_spec = pl.BlockSpec((group, 3 * W, HD), lambda s, window: (s, 0, 0))
        asked_specs, out_specs = [q_spec] * 2, [o_spec] * 2
        out_shape = [jax.ShapeDtypeStruct((count + 1, 3 * W, HD), BF16)] * 2
    else:
        asked_specs = [heads, gains, norms]
        out_specs = [
            pl.BlockSpec((group, 2, 3, W, HD), lambda s, window: (s, 0, 0, 0, 0)),
            whole((2, 3 * W, HD)),
        ]
        out_shape = [
            jax.ShapeDtypeStruct((count, 2, 3, W, HD), BF16),
            jax.ShapeDtypeStruct((2, 3 * W, HD), F32),
        ]
    return pl.pallas_call(
        functools.partial(partial_kernel, far, start, group, steps),
        grid_spec=pltpu.PrefetchScalarGridSpec(
            num_scalar_prefetch=1,
            grid=(steps + 1 if far else steps,),
            in_specs=[norms, heads, heads, gains, rows, rows] + asked_specs,
            out_specs=out_specs,
            scratch_shapes=line_scratch(group)
            + [pltpu.VMEM((2, 3, W, 3 * W), jnp.int32), pltpu.VMEM((2, 2, 3 * W, HD), F32)],
        ),
        out_shape=out_shape,
        compiler_params=params(16),
        cost_estimate=cost(0.6 * count),
        name="far_partial" if far else "own_partial",
    )(window, kinverse, k, v, kgain, low, high, *asked)


def far_partial(window, queries, k, v, kgain, kinverse, rows, start, count):
    return partial_call(True, window, k, v, kgain, kinverse, *rows, queries, start, count)


def own_partial(window, q, k, v, qgain, kgain, qinverse, kinverse, rows, start, count):
    return partial_call(False, window, k, v, kgain, kinverse, *rows, (q, qgain, qinverse), start, count)


def merge_kernel(start, group, window, part, lse, ob, oa, sb, sa, *refs):
    out, shares = refs[-2:]
    lane = lax.broadcasted_iota(jnp.int32, (3 * W, HD), 1)
    neighbours = inside("frame")
    step = pl.program_id(0)

    @pl.when(step == 0)
    def _():
        for j, st in enumerate(sides("frame", sb[0], sa[0])):
            pieces = st.astype(F32)
            other = pieces + pltpu.roll(pieces, HD - 32, 1) + pltpu.roll(pieces, HD - 64, 1)
            other = jnp.where(neighbours[j], other, NEG)
            top = jnp.maximum(lse[j], other)
            own_weight = jnp.exp2(lse[j] - top)
            other_weight = jnp.exp2(other - top)
            shares[j] = other_weight / (own_weight + other_weight)

    for g in range(group):
        here = lane == step * group + g
        for j, far in enumerate(sides("frame", ob[g], oa[g])):
            share = jnp.sum(jnp.where(here, shares[j], 0.0), axis=1, keepdims=True)
            share = jnp.where(window[start + step * group + g, 0] > 0, share, 0.0)
            own = part[g, j].reshape(3 * W, HD).astype(F32)
            mixed = own + (far.astype(F32) - own) * share
            out[j, :, :, lanes(g)] = mixed.astype(BF16).reshape(3, W, HD)


def merge(window, out, part, lse, o_below, o_above, start, count):
    group = group_of(start, count)
    o_spec = pl.BlockSpec((group, 3 * W, HD), lambda s, window: (s, 0, 0))
    stat_spec = pl.BlockSpec((1, 3 * W, HD), lambda s, window: (count, 0, 0))
    return pl.pallas_call(
        functools.partial(merge_kernel, start, group),
        grid_spec=pltpu.PrefetchScalarGridSpec(
            num_scalar_prefetch=1,
            grid=(count // group,),
            in_specs=[
                pl.BlockSpec((group, 2, 3, W, HD), lambda s, window: (s, 0, 0, 0, 0)),
                whole((2, 3 * W, HD)),
                o_spec,
                o_spec,
                stat_spec,
                stat_spec,
            ]
            + ([] if out is None else [pl.BlockSpec(memory_space=pl.ANY)]),
            out_specs=heads_spec(start, group),
            scratch_shapes=[pltpu.VMEM((2, 3 * W, HD), F32)],
        ),
        out_shape=jax.ShapeDtypeStruct((2, 3, W, NH * HD), BF16),
        input_output_aliases={} if out is None else {7: 0},
        compiler_params=params(),
        cost_estimate=cost(0.25 * count),
        name="merge",
    )(window, part, lse, o_below, o_above, o_below, o_above, *([] if out is None else [out]))


def exchange(axis, first, second):
    out = []
    for start, block in enumerate((first, second)):
        pairs = [(i, i + 1) for i in range(start, lax.axis_size(axis) - 1, 2)]
        out.append(lax.ppermute(block, axis, pairs + [(b, a) for a, b in pairs]))
    return out


def attention(window, q, k, v, q_gain, k_gain, q_inverse, k_inverse):
    norms = (q_gain, k_gain, q_inverse, k_inverse)
    chunks = ((0, FIRST), (FIRST, NH - FIRST))
    queries, rows = [], []
    for start, count in chunks:
        packed = pack_queries(window, q, q_gain, q_inverse, start, count)
        k, *packed = lax.optimization_barrier((k, *packed))
        if queries:
            *packed, queries[0][0], queries[0][1] = lax.optimization_barrier((*packed, *queries[0]))
        packed_rows = pack_rows(window, k, v, k_gain, k_inverse, start, count)
        rows.append(exchange("height", *packed_rows))
        queries.append(exchange("frame", *packed))
        q, *_ = lax.optimization_barrier((q, *packed_rows))
    parts = []
    for n, (start, count) in enumerate(chunks):
        far = far_partial(window, queries[n], k, v, k_gain, k_inverse, rows[n], start, count)
        q, *queries[1] = lax.optimization_barrier((q, *queries[1]))
        part, lse = own_partial(window, q, k, v, *norms, rows[n], start, count)
        k, part = lax.optimization_barrier((k, part))
        parts.append((part, lse, *exchange("frame", *far), start, count))
    out = None
    for part in parts:
        out = merge(window, out, *part)
    return out


def squares_of(raw):
    values = raw.astype(F32)
    return jnp.sum(values * values, axis=-1)


def body(q, k, v, q_gain, k_gain, window):
    width_total = q.shape[3] * lax.axis_size("head")
    query_sum, key_sum = lax.psum((squares_of(q), squares_of(k)), "head")

    def inverse_of(total):
        return jnp.broadcast_to(lax.rsqrt(total / width_total + EPS)[..., None], (2, 3, W, HD))

    return attention(
        window, q, k, v, q_gain[None], k_gain[None], inverse_of(query_sum), inverse_of(key_sum)
    )


def solution(mesh):
    placed = (
        P("frame", "height", None, "head"),
        P("frame", "height", None, "head"),
        P("frame", "height", None, "head"),
        P("head"),
        P("head"),
        P("head", None),
    )
    return jax.shard_map(
        body,
        mesh=mesh,
        in_specs=placed,
        out_specs=P("frame", "height", None, "head"),
        check_vma=False,
    )
```

```python
import functools
import math

import jax
import jax.numpy as jnp
from jax import lax
from jax.experimental import pallas as pl
from jax.experimental.pallas import tpu as pltpu
from jax.sharding import PartitionSpec as P

HD = 128
W = 80
NH = 20
FIRST = 10
EPS = 1e-06
NEG = -1e30
FAR = 100
LOG2E = math.log2(math.e)
SCALE2 = LOG2E / math.sqrt(HD)
F32 = jnp.float32
BF16 = jnp.bfloat16


def params(mib=12):
    return pltpu.CompilerParams(vmem_limit_bytes=mib * 1024 * 1024)


def cost(microseconds):
    return pl.CostEstimate(flops=0, bytes_accessed=int(microseconds * 3_000_000), transcendentals=0)


def normed(raw, inverse, gain):
    return (raw.astype(F32) * inverse * gain).astype(BF16)


def lanes(g):
    return slice(g * HD, (g + 1) * HD)


def heads_spec(start, group):
    return pl.BlockSpec((2, 3, W, group * HD), lambda s, window: (0, 0, 0, start // group + s))


def gains_spec(start, group):
    return pl.BlockSpec((1, group * HD), lambda s, window: (0, start // group + s))


def whole(shape):
    return pl.BlockSpec(shape, lambda s, window: (0,) * len(shape))


def pack_queries_kernel(group, window, raw, gain, inverse, first, second):
    for g in range(group):
        q = normed(raw[:, :, :, lanes(g)], inverse[...], gain[:, lanes(g)].reshape(1, 1, 1, HD))
        first[g], second[g] = sides("frame", q[0].reshape(3 * W, HD), q[1].reshape(3 * W, HD))


def pack_rows_kernel(group, window, keys, values, gain, inverse, first, second):
    for g in range(group):
        k_gain = gain[:, lanes(g)].reshape(1, 1, HD)
        for n, row_of in (
            (0, lambda row: normed(keys[:, row, :, lanes(g)], inverse[:, row], k_gain)),
            (1, lambda row: values[:, row, :, lanes(g)]),
        ):
            first[g, n], second[g, n] = sides("height", row_of(0), row_of(2))


def group_of(start, count):
    return max(n for n in (1, 2, 4, 5) if count % n == 0 and start % n == 0)


def pack_queries(window, q, gain, inverse, start, count):
    group = group_of(start, count)
    out = jax.ShapeDtypeStruct((count, 3 * W, HD), BF16)
    out_spec = pl.BlockSpec((group, 3 * W, HD), lambda s, window: (s, 0, 0))
    return pl.pallas_call(
        functools.partial(pack_queries_kernel, group),
        grid_spec=pltpu.PrefetchScalarGridSpec(
            num_scalar_prefetch=1,
            grid=(count // group,),
            in_specs=[heads_spec(start, group), gains_spec(start, group), whole((2, 3, W, HD))],
            out_specs=[out_spec, out_spec],
        ),
        out_shape=[out, out],
        compiler_params=params(),
        cost_estimate=cost(0.1 * count),
        name="pack_queries",
    )(window, q, gain, inverse)


def pack_rows(window, k, v, gain, inverse, start, count):
    group = group_of(start, count)
    out = jax.ShapeDtypeStruct((count, 2, 2, W, HD), BF16)
    out_spec = pl.BlockSpec((group, 2, 2, W, HD), lambda s, window: (s, 0, 0, 0, 0))
    return pl.pallas_call(
        functools.partial(pack_rows_kernel, group),
        grid_spec=pltpu.PrefetchScalarGridSpec(
            num_scalar_prefetch=1,
            grid=(count // group,),
            in_specs=[heads_spec(start, group)] * 2 + [gains_spec(start, group), whole((2, 3, W, HD))],
            out_specs=[out_spec, out_spec],
        ),
        out_shape=[out, out],
        compiler_params=params(),
        cost_estimate=cost(0.15 * count),
        name="pack_rows",
    )(window, k, v, gain, inverse)


def fill_lines(kx, vx, k, v, inverse, gain, first, second):
    kn = normed(k, inverse, gain.reshape(1, 1, 1, HD))
    low, high = sides("height", first[...], second[...])
    for j in range(2):
        kx[j, 0:W] = low[0, j]
        kx[j, W : 4 * W] = kn[j].reshape(3 * W, HD)
        kx[j, 4 * W : 5 * W] = high[0, j]
        vx[j, 0:W, 0:HD] = low[1, j]
        vx[j, W : 4 * W, 0:HD] = v[j].reshape(3 * W, HD)
        vx[j, 4 * W : 5 * W, 0:HD] = high[1, j]


def line_scratch(group):
    return [pltpu.VMEM((2, 5 * W, HD), BF16)] * group + [pltpu.VMEM((2, 5 * W, 2 * HD), BF16)] * group


def even(axis):
    return lax.rem(lax.axis_index(axis), 2) == 0


def sides(axis, first, second):
    return jnp.where(even(axis), second, first), jnp.where(even(axis), first, second)


def inside(axis):
    at = lax.axis_index(axis)
    return at > 0, at < lax.axis_size(axis) - 1


def fill_ones(values):
    for vx in values:
        vx[:, :, HD:] = jnp.ones((2, 5 * W, HD), BF16)


def fill_gaps(gaps):
    lane = lax.broadcasted_iota(jnp.int32, (W, 3 * W), 1)
    line = (lane >= W).astype(jnp.int32) + (lane >= 2 * W).astype(jnp.int32)
    key_tile = (lane - W * line) >> 3
    query_tile = lax.broadcasted_iota(jnp.int32, (W, 3 * W), 0) >> 3
    gap = jnp.abs(key_tile - query_tile)
    below, above = inside("height")
    no_low = jnp.where(below, 0, FAR)
    no_high = jnp.where(above, 0, FAR)
    for reach in range(2):
        for i in range(3):
            low = FAR if reach == 0 else (no_low if i == 0 else 0)
            high = FAR if reach == 0 else (no_high if i == 2 else 0)
            gaps[reach, i] = gap + jnp.where(line == 0, low, 0) + jnp.where(line == 2, high, 0)


def biases(gaps, window, head):
    reach_row, reach_tile = jnp.minimum(window[head, 1], 1), window[head, 2]
    return [jnp.where(gaps[reach_row, i] <= reach_tile, 0.0, NEG).astype(F32) for i in range(3)]


def dot_t(q, k):
    return lax.dot_general(q, k, (((1,), (1,)), ((), ())), preferred_element_type=F32)


def lines_of(i):
    return slice(i * W, (i + 3) * W)


def row_max(s):
    return jnp.max(s, axis=-1, keepdims=True)


def weights_of(s, top):
    return jnp.exp2((s - top) * SCALE2).astype(BF16)


def divided(mixed):
    total = mixed[:, HD:]
    inverse = pl.reciprocal(total, approx=True)
    inverse = inverse * (2.0 - total * inverse)
    return (mixed[:, :HD] * inverse).astype(BF16)


def mark(st, at, here, top, mixed):
    st[0, at] = jnp.where(here, top, st[0, at])
    st[1, at] = jnp.where(here, mixed[:, HD:], st[1, at])


def lse_of(st):
    return st[0] * SCALE2 + jnp.log(st[1]) * LOG2E


def pieces_of(full, lane):
    high = full.astype(BF16).astype(F32)
    rest = full - high
    middle = rest.astype(BF16).astype(F32)
    low = rest - middle
    return jnp.where(lane < 32, high, jnp.where(lane < 64, middle, jnp.where(lane < 96, low, 0.0))).astype(BF16)


def partial_kernel(far, start, group, steps, window, kinverse, k, v, kgain, low, high, *refs):
    if far:
        qb, qa, ob, oa = refs[:4]
    else:
        q, qgain, qinverse, part, own_stats = refs[:5]
    kxs, vxs = refs[-2 - 2 * group : -2 - group], refs[-2 - group : -2]
    gaps, st = refs[-2:]
    step = pl.program_id(0)

    @pl.when(step == 0)
    def _():
        for j in range(2):
            st[j, 0] = jnp.zeros((3 * W, HD), F32)
            st[j, 1] = jnp.ones((3 * W, HD), F32)
        fill_ones(vxs)
        fill_gaps(gaps)

    @pl.when(step < steps)
    def _():
        for g in range(group):
            own_keys, own_values = k[:, :, :, lanes(g)], v[:, :, :, lanes(g)]
            fill_lines(
                kxs[g], vxs[g], own_keys, own_values, kinverse[...], kgain[:, lanes(g)], low.at[g], high.at[g]
            )
        if far:
            far_step(start, group, step, window, qb, qa, ob, oa, kxs, vxs, gaps, st)
        else:
            own_step(start, group, step, window, q, qgain, qinverse, part, kxs, vxs, gaps, st)

    if far:

        @pl.when(step == steps)
        def _():
            lane = lax.broadcasted_iota(jnp.int32, (3 * W, HD), 1)
            below, above = (pieces_of(lse_of(st[j]), lane) for j in range(2))
            ob[0], oa[0] = sides("frame", below, above)

    else:

        @pl.when(step == steps - 1)
        def _():
            for j in range(2):
                own_stats[j] = lse_of(st[j])


def marked_lanes(step, group, g):
    return (lax.broadcasted_iota(jnp.int32, (W, HD), 1) & 31) == step * group + g


def far_step(start, group, step, window, qb, qa, ob, oa, kxs, vxs, gaps, st):
    scores = []
    for g in range(group):
        masks = biases(gaps, window, start + step * group + g)
        for i in range(3):
            at = slice(i * W, (i + 1) * W)
            asked = sides("frame", qb[g, at], qa[g, at])
            scores += [dot_t(asked[j], kxs[g][j, lines_of(i)]) + masks[i] for j in range(2)]
    tops = [row_max(s) for s in scores]
    weights = [weights_of(s, top) for s, top in zip(scores, tops)]
    for g in range(group):
        here = marked_lanes(step, group, g)
        for i in range(3):
            at, n = slice(i * W, (i + 1) * W), 6 * g + 2 * i
            mixed = [
                jnp.dot(weights[n + j], vxs[g][j, lines_of(i)], preferred_element_type=F32) for j in range(2)
            ]
            for j in range(2):
                mark(st.at[j], at, here, tops[n + j], mixed[j])
            ob[g, at], oa[g, at] = sides("frame", divided(mixed[0]), divided(mixed[1]))


def own_step(start, group, step, window, q, qgain, qinverse, part, kxs, vxs, gaps, st):
    scores = []
    for g in range(group):
        head = start + step * group + g
        masks = biases(gaps, window, head)
        cross = jnp.where(window[head, 0] > 0, 0.0, NEG)
        qn = normed(q[:, :, :, lanes(g)], qinverse[...], qgain[:, lanes(g)].reshape(1, 1, 1, HD))
        for i in range(3):
            own = qn[:, i].reshape(2 * W, HD)
            other = masks[i] + cross
            for j in range(2):
                raw = dot_t(own, kxs[g][j, lines_of(i)])
                order = (masks[i], other) if j == 0 else (other, masks[i])
                scores.append([raw[W * n : W * (n + 1)] + order[n] for n in range(2)])
    tops, weights = [], []
    for s0, s1 in zip(scores[::2], scores[1::2]):
        top = [row_max(jnp.maximum(s0[n], s1[n])) for n in range(2)]
        tops.append(top)
        for s in (s0, s1):
            weights.append(jnp.concatenate([weights_of(a, b) for a, b in zip(s, top)], axis=0))
    for g in range(group):
        here = marked_lanes(step, group, g)
        for i in range(3):
            at, n = slice(i * W, (i + 1) * W), 3 * g + i
            m0, m1 = (
                jnp.dot(weights[2 * n + j], vxs[g][j, lines_of(i)], preferred_element_type=F32)
                for j in range(2)
            )
            for f in range(2):
                own = m0[W * f : W * (f + 1)] + m1[W * f : W * (f + 1)]
                part[g, f, i] = divided(own)
                mark(st.at[f], at, here, tops[n][f], own)


def partial_call(far, window, k, v, kgain, kinverse, low, high, asked, start, count):
    group = 2
    steps = count // group

    def step_of(s):
        return jnp.minimum(s, steps - 1)

    heads = pl.BlockSpec((2, 3, W, group * HD), lambda s, window: (0, 0, 0, start // group + step_of(s)))
    gains = pl.BlockSpec((1, group * HD), lambda s, window: (0, start // group + step_of(s)))
    rows = pl.BlockSpec((group, 2, 2, W, HD), lambda s, window: (step_of(s), 0, 0, 0, 0))
    norms = whole((2, 3, W, HD))
    if far:
        q_spec = pl.BlockSpec((group, 3 * W, HD), lambda s, window: (step_of(s), 0, 0))
        o_spec = pl.BlockSpec((group, 3 * W, HD), lambda s, window: (s, 0, 0))
        asked_specs, out_specs = [q_spec] * 2, [o_spec] * 2
        out_shape = [jax.ShapeDtypeStruct((count + 1, 3 * W, HD), BF16)] * 2
    else:
        asked_specs = [heads, gains, norms]
        out_specs = [
            pl.BlockSpec((group, 2, 3, W, HD), lambda s, window: (s, 0, 0, 0, 0)),
            whole((2, 3 * W, HD)),
        ]
        out_shape = [
            jax.ShapeDtypeStruct((count, 2, 3, W, HD), BF16),
            jax.ShapeDtypeStruct((2, 3 * W, HD), F32),
        ]
    return pl.pallas_call(
        functools.partial(partial_kernel, far, start, group, steps),
        grid_spec=pltpu.PrefetchScalarGridSpec(
            num_scalar_prefetch=1,
            grid=(steps + 1 if far else steps,),
            in_specs=[norms, heads, heads, gains, rows, rows] + asked_specs,
            out_specs=out_specs,
            scratch_shapes=line_scratch(group)
            + [pltpu.VMEM((2, 3, W, 3 * W), jnp.int32), pltpu.VMEM((2, 2, 3 * W, HD), F32)],
        ),
        out_shape=out_shape,
        compiler_params=params(16),
        cost_estimate=cost(0.6 * count),
        name="far_partial" if far else "own_partial",
    )(window, kinverse, k, v, kgain, low, high, *asked)


def far_partial(window, queries, k, v, kgain, kinverse, rows, start, count):
    return partial_call(True, window, k, v, kgain, kinverse, *rows, queries, start, count)


def own_partial(window, q, k, v, qgain, kgain, qinverse, kinverse, rows, start, count):
    return partial_call(False, window, k, v, kgain, kinverse, *rows, (q, qgain, qinverse), start, count)


def both_kernel(start, group, steps, window, *refs):
    st_own, st_far = refs[-2:]
    ob, oa, own_stats = refs[-6 - 2 * group : -3 - 2 * group]
    step = pl.program_id(0)

    @pl.when(step < steps)
    def _():
        both_step(start, group, step, window, *refs)

    @pl.when(step == steps)
    def _():
        lane = lax.broadcasted_iota(jnp.int32, (3 * W, HD), 1)
        for j in range(2):
            own_stats[j] = lse_of(st_own[j])
        below, above = (pieces_of(lse_of(st_far[j]), lane) for j in range(2))
        ob[0], oa[0] = sides("frame", below, above)


def both_step(start, group, step, window, *refs):
    qinverse, kinverse, qb, qa, q, k, v, qgain, kgain, low, high, part, ob, oa, _ = refs[:15]
    kxs, vxs = refs[15 : 15 + group], refs[15 + group : 15 + 2 * group]
    gaps, st_own, st_far = refs[-3:]
    slot = start + step * group

    @pl.when(step == 0)
    def _():
        for st in (st_own, st_far):
            for j in range(2):
                st[j, 0] = jnp.zeros((3 * W, HD), F32)
                st[j, 1] = jnp.ones((3 * W, HD), F32)
        fill_ones(vxs)
        fill_gaps(gaps)

    scores = []
    for g in range(group):
        own_keys, own_values = k[:, :, :, lanes(g)], v[:, :, :, lanes(g)]
        fill_lines(kxs[g], vxs[g], own_keys, own_values, kinverse[...], kgain[:, lanes(g)], low.at[g], high.at[g])
        masks = biases(gaps, window, slot + g)
        cross = jnp.where(window[slot + g, 0] > 0, 0.0, NEG)
        qn = normed(q[:, :, :, lanes(g)], qinverse[...], qgain[:, lanes(g)].reshape(1, 1, 1, HD))
        for i in range(3):
            own = qn[:, i].reshape(2 * W, HD)
            far = masks[i] + cross
            asked = sides("frame", qb[g, i * W : (i + 1) * W], qa[g, i * W : (i + 1) * W])
            for j in range(2):
                queries = jnp.concatenate([own, asked[j]], axis=0)
                order = [masks[i], far, masks[i]] if j == 0 else [far, masks[i], masks[i]]
                raw = dot_t(queries, kxs[g][j, lines_of(i)])
                scores.append([raw[W * n : W * (n + 1)] + order[n] for n in range(3)])
    tops, weights = [], []
    for s0, s1 in zip(scores[::2], scores[1::2]):
        first, second = (row_max(jnp.maximum(s0[n], s1[n])) for n in range(2))
        below, above = row_max(s0[2]), row_max(s1[2])
        tops.append((jnp.concatenate([first, second], axis=0), below, above))
        for s, last in ((s0, below), (s1, above)):
            parts = [weights_of(a, b) for a, b in zip(s, (first, second, last))]
            weights.append(jnp.concatenate(parts, axis=0))
    lane = lax.broadcasted_iota(jnp.int32, (W, HD), 1)
    for g in range(group):
        here = (lane & 31) == step * group + g
        for i in range(3):
            w0, w1 = weights[6 * g + 2 * i : 6 * g + 2 * i + 2]
            top, top_b, top_a = tops[3 * g + i]
            m0 = jnp.dot(w0, vxs[g][0, lines_of(i)], preferred_element_type=F32)
            m1 = jnp.dot(w1, vxs[g][1, lines_of(i)], preferred_element_type=F32)
            at = slice(i * W, (i + 1) * W)
            for n in range(2):
                own = m0[W * n : W * (n + 1)] + m1[W * n : W * (n + 1)]
                part[g, n, i] = divided(own)
                mark(st_own.at[n], at, here, top[W * n : W * (n + 1)], own)
            for n, far in ((0, m0[2 * W :]), (1, m1[2 * W :])):
                mark(st_far.at[n], at, here, (top_b, top_a)[n], far)
            ob[g, at], oa[g, at] = sides("frame", divided(m0[2 * W :]), divided(m1[2 * W :]))


def both_partial(window, qb, qa, q, k, v, qgain, kgain, qinverse, kinverse, low, high, start, count):
    group = 2
    steps = count // group

    def step_of(s):
        return jnp.minimum(s, steps - 1)

    heads = pl.BlockSpec((2, 3, W, group * HD), lambda s, window: (0, 0, 0, start // group + step_of(s)))
    gains = pl.BlockSpec((1, group * HD), lambda s, window: (0, start // group + step_of(s)))
    rows = pl.BlockSpec((group, 2, 2, W, HD), lambda s, window: (step_of(s), 0, 0, 0, 0))
    q_spec = pl.BlockSpec((group, 3 * W, HD), lambda s, window: (step_of(s), 0, 0))
    o_spec = pl.BlockSpec((group, 3 * W, HD), lambda s, window: (s, 0, 0))
    out = jax.ShapeDtypeStruct((count + 1, 3 * W, HD), BF16)
    stat = pltpu.VMEM((2, 2, 3 * W, HD), F32)
    return pl.pallas_call(
        functools.partial(both_kernel, start, group, steps),
        grid_spec=pltpu.PrefetchScalarGridSpec(
            num_scalar_prefetch=1,
            grid=(steps + 1,),
            in_specs=[whole((2, 3, W, HD))] * 2 + [q_spec] * 2 + [heads] * 3 + [gains] * 2 + [rows] * 2,
            out_specs=[
                pl.BlockSpec((group, 2, 3, W, HD), lambda s, window: (step_of(s), 0, 0, 0, 0)),
                o_spec,
                o_spec,
                whole((2, 3 * W, HD)),
            ],
            scratch_shapes=line_scratch(group) + [pltpu.VMEM((2, 3, W, 3 * W), jnp.int32), stat, stat],
        ),
        out_shape=[
            jax.ShapeDtypeStruct((count, 2, 3, W, HD), BF16),
            out,
            out,
            jax.ShapeDtypeStruct((2, 3 * W, HD), F32),
        ],
        compiler_params=params(16),
        cost_estimate=cost(1.1 * count),
        name="both_partial",
    )(window, qinverse, kinverse, qb, qa, q, k, v, qgain, kgain, low, high)


def merge_kernel(start, group, window, part, lse, ob, oa, sb, sa, *refs):
    out, shares = refs[-2:]
    lane = lax.broadcasted_iota(jnp.int32, (3 * W, HD), 1)
    neighbours = inside("frame")
    step = pl.program_id(0)

    @pl.when(step == 0)
    def _():
        for j, st in enumerate(sides("frame", sb[0], sa[0])):
            pieces = st.astype(F32)
            other = pieces + pltpu.roll(pieces, HD - 32, 1) + pltpu.roll(pieces, HD - 64, 1)
            other = jnp.where(neighbours[j], other, NEG)
            top = jnp.maximum(lse[j], other)
            own_weight = jnp.exp2(lse[j] - top)
            other_weight = jnp.exp2(other - top)
            shares[j] = other_weight / (own_weight + other_weight)

    for g in range(group):
        here = lane == step * group + g
        for j, far in enumerate(sides("frame", ob[g], oa[g])):
            share = jnp.sum(jnp.where(here, shares[j], 0.0), axis=1, keepdims=True)
            share = jnp.where(window[start + step * group + g, 0] > 0, share, 0.0)
            own = part[g, j].reshape(3 * W, HD).astype(F32)
            mixed = own + (far.astype(F32) - own) * share
            out[j, :, :, lanes(g)] = mixed.astype(BF16).reshape(3, W, HD)


def merge(window, out, part, lse, o_below, o_above, start, count):
    group = group_of(start, count)
    o_spec = pl.BlockSpec((group, 3 * W, HD), lambda s, window: (s, 0, 0))
    stat_spec = pl.BlockSpec((1, 3 * W, HD), lambda s, window: (count, 0, 0))
    return pl.pallas_call(
        functools.partial(merge_kernel, start, group),
        grid_spec=pltpu.PrefetchScalarGridSpec(
            num_scalar_prefetch=1,
            grid=(count // group,),
            in_specs=[
                pl.BlockSpec((group, 2, 3, W, HD), lambda s, window: (s, 0, 0, 0, 0)),
                whole((2, 3 * W, HD)),
                o_spec,
                o_spec,
                stat_spec,
                stat_spec,
            ]
            + ([] if out is None else [pl.BlockSpec(memory_space=pl.ANY)]),
            out_specs=heads_spec(start, group),
            scratch_shapes=[pltpu.VMEM((2, 3 * W, HD), F32)],
        ),
        out_shape=jax.ShapeDtypeStruct((2, 3, W, NH * HD), BF16),
        input_output_aliases={} if out is None else {7: 0},
        compiler_params=params(),
        cost_estimate=cost(0.25 * count),
        name="merge",
    )(window, part, lse, o_below, o_above, o_below, o_above, *([] if out is None else [out]))


def exchange(axis, first, second):
    out = []
    for start, block in enumerate((first, second)):
        pairs = [(i, i + 1) for i in range(start, lax.axis_size(axis) - 1, 2)]
        out.append(lax.ppermute(block, axis, pairs + [(b, a) for a, b in pairs]))
    return out


def attention(window, q, k, v, q_gain, k_gain, q_inverse, k_inverse):
    norms = (q_gain, k_gain, q_inverse, k_inverse)
    chunks = ((0, FIRST), (FIRST, NH - FIRST))
    queries, rows = [], []
    for start, count in chunks:
        packed = pack_queries(window, q, q_gain, q_inverse, start, count)
        k, *packed = lax.optimization_barrier((k, *packed))
        packed_rows = pack_rows(window, k, v, k_gain, k_inverse, start, count)
        rows.append(exchange("height", *packed_rows))
        queries.append(exchange("frame", *packed))
        q, *_ = lax.optimization_barrier((q, *packed_rows))
    (start, count), (late_start, late_count) = chunks
    part, *far, lse = both_partial(window, *queries[0], q, k, v, *norms, *rows[0], start, count)
    parts = [(part, lse, *exchange("frame", *far), start, count)]
    far = far_partial(window, queries[1], k, v, k_gain, k_inverse, rows[1], late_start, late_count)
    part, lse = own_partial(window, q, k, v, *norms, rows[1], late_start, late_count)
    parts.append((part, lse, *exchange("frame", *far), late_start, late_count))
    out = None
    for part in parts:
        out = merge(window, out, *part)
    return out


def squares_of(raw):
    values = raw.astype(F32)
    return jnp.sum(values * values, axis=-1)


def body(q, k, v, q_gain, k_gain, window):
    width_total = q.shape[3] * lax.axis_size("head")
    query_sum, key_sum = lax.psum((squares_of(q), squares_of(k)), "head")

    def inverse_of(total):
        return jnp.broadcast_to(lax.rsqrt(total / width_total + EPS)[..., None], (2, 3, W, HD))

    return attention(
        window, q, k, v, q_gain[None], k_gain[None], inverse_of(query_sum), inverse_of(key_sum)
    )


def solution(mesh):
    placed = (
        P("frame", "height", None, "head"),
        P("frame", "height", None, "head"),
        P("frame", "height", None, "head"),
        P("head"),
        P("head"),
        P("head", None),
    )
    return jax.shard_map(
        body,
        mesh=mesh,
        in_specs=placed,
        out_specs=P("frame", "height", None, "head"),
        check_vma=False,
    )
```

```python
import functools
import math

import jax
import jax.numpy as jnp
from jax import lax
from jax.experimental import pallas as pl
from jax.experimental.pallas import tpu as pltpu
from jax.sharding import PartitionSpec as P

HD = 128
W = 80
NH = 20
FIRST = 10
EPS = 1e-06
NEG = -1e30
FAR = 100
LOG2E = math.log2(math.e)
SCALE2 = LOG2E / math.sqrt(HD)
F32 = jnp.float32
BF16 = jnp.bfloat16


def params(mib=12):
    return pltpu.CompilerParams(vmem_limit_bytes=mib * 1024 * 1024)


def cost(microseconds):
    return pl.CostEstimate(flops=0, bytes_accessed=int(microseconds * 3_000_000), transcendentals=0)


def normed(raw, inverse, gain):
    return (raw.astype(F32) * inverse * gain).astype(BF16)


def lanes(g):
    return slice(g * HD, (g + 1) * HD)


def heads_spec(start, group):
    return pl.BlockSpec((2, 3, W, group * HD), lambda s, window: (0, 0, 0, start // group + s))


def gains_spec(start, group):
    return pl.BlockSpec((1, group * HD), lambda s, window: (0, start // group + s))


def whole(shape):
    return pl.BlockSpec(shape, lambda s, window: (0,) * len(shape))


def pack_queries_kernel(group, window, raw, gain, inverse, first, second):
    for g in range(group):
        q = normed(raw[:, :, :, lanes(g)], inverse[...], gain[:, lanes(g)].reshape(1, 1, 1, HD))
        first[g], second[g] = sides("frame", q[0].reshape(3 * W, HD), q[1].reshape(3 * W, HD))


def pack_rows_kernel(group, window, keys, values, gain, inverse, first, second):
    for g in range(group):
        k_gain = gain[:, lanes(g)].reshape(1, 1, HD)
        for n, row_of in (
            (0, lambda row: normed(keys[:, row, :, lanes(g)], inverse[:, row], k_gain)),
            (1, lambda row: values[:, row, :, lanes(g)]),
        ):
            first[g, n], second[g, n] = sides("height", row_of(0), row_of(2))


def group_of(start, count):
    return max(n for n in (1, 2, 4, 5) if count % n == 0 and start % n == 0)


def pack_queries(window, q, gain, inverse, start, count):
    group = group_of(start, count)
    out = jax.ShapeDtypeStruct((count, 3 * W, HD), BF16)
    out_spec = pl.BlockSpec((group, 3 * W, HD), lambda s, window: (s, 0, 0))
    return pl.pallas_call(
        functools.partial(pack_queries_kernel, group),
        grid_spec=pltpu.PrefetchScalarGridSpec(
            num_scalar_prefetch=1,
            grid=(count // group,),
            in_specs=[heads_spec(start, group), gains_spec(start, group), whole((2, 3, W, HD))],
            out_specs=[out_spec, out_spec],
        ),
        out_shape=[out, out],
        compiler_params=params(),
        cost_estimate=cost(0.1 * count),
        name="pack_queries",
    )(window, q, gain, inverse)


def pack_rows(window, k, v, gain, inverse, start, count):
    group = group_of(start, count)
    out = jax.ShapeDtypeStruct((count, 2, 2, W, HD), BF16)
    out_spec = pl.BlockSpec((group, 2, 2, W, HD), lambda s, window: (s, 0, 0, 0, 0))
    return pl.pallas_call(
        functools.partial(pack_rows_kernel, group),
        grid_spec=pltpu.PrefetchScalarGridSpec(
            num_scalar_prefetch=1,
            grid=(count // group,),
            in_specs=[heads_spec(start, group)] * 2 + [gains_spec(start, group), whole((2, 3, W, HD))],
            out_specs=[out_spec, out_spec],
        ),
        out_shape=[out, out],
        compiler_params=params(),
        cost_estimate=cost(0.15 * count),
        name="pack_rows",
    )(window, k, v, gain, inverse)


def fill_lines(kx, vx, k, v, inverse, gain, first, second):
    kn = normed(k, inverse, gain.reshape(1, 1, 1, HD))
    low, high = sides("height", first[...], second[...])
    for j in range(2):
        kx[j, 0:W] = low[0, j]
        kx[j, W : 4 * W] = kn[j].reshape(3 * W, HD)
        kx[j, 4 * W : 5 * W] = high[0, j]
        vx[j, 0:W, 0:HD] = low[1, j]
        vx[j, W : 4 * W, 0:HD] = v[j].reshape(3 * W, HD)
        vx[j, 4 * W : 5 * W, 0:HD] = high[1, j]


def line_scratch(group):
    return [pltpu.VMEM((2, 5 * W, HD), BF16)] * group + [pltpu.VMEM((2, 5 * W, 2 * HD), BF16)] * group


def even(axis):
    return lax.rem(lax.axis_index(axis), 2) == 0


def sides(axis, first, second):
    return jnp.where(even(axis), second, first), jnp.where(even(axis), first, second)


def inside(axis):
    at = lax.axis_index(axis)
    return at > 0, at < lax.axis_size(axis) - 1


def fill_ones(values):
    for vx in values:
        vx[:, :, HD:] = jnp.ones((2, 5 * W, HD), BF16)


def fill_gaps(gaps):
    lane = lax.broadcasted_iota(jnp.int32, (W, 3 * W), 1)
    line = (lane >= W).astype(jnp.int32) + (lane >= 2 * W).astype(jnp.int32)
    key_tile = (lane - W * line) >> 3
    query_tile = lax.broadcasted_iota(jnp.int32, (W, 3 * W), 0) >> 3
    gap = jnp.abs(key_tile - query_tile)
    below, above = inside("height")
    no_low = jnp.where(below, 0, FAR)
    no_high = jnp.where(above, 0, FAR)
    for reach in range(2):
        for i in range(3):
            low = FAR if reach == 0 else (no_low if i == 0 else 0)
            high = FAR if reach == 0 else (no_high if i == 2 else 0)
            gaps[reach, i] = gap + jnp.where(line == 0, low, 0) + jnp.where(line == 2, high, 0)


def biases(gaps, window, head):
    reach_row, reach_tile = jnp.minimum(window[head, 1], 1), window[head, 2]
    return [jnp.where(gaps[reach_row, i] <= reach_tile, 0.0, NEG).astype(F32) for i in range(3)]


def dot_t(q, k):
    return lax.dot_general(q, k, (((1,), (1,)), ((), ())), preferred_element_type=F32)


def lines_of(i):
    return slice(i * W, (i + 3) * W)


def row_max(s):
    return jnp.max(s, axis=-1, keepdims=True)


def weights_of(s, top):
    return jnp.exp2((s - top) * SCALE2).astype(BF16)


def divided(mixed):
    total = mixed[:, HD:]
    inverse = pl.reciprocal(total, approx=True)
    inverse = inverse * (2.0 - total * inverse)
    return (mixed[:, :HD] * inverse).astype(BF16)


def mark(st, at, here, top, mixed):
    st[0, at] = jnp.where(here, top, st[0, at])
    st[1, at] = jnp.where(here, mixed[:, HD:], st[1, at])


def lse_of(st):
    return st[0] * SCALE2 + jnp.log(st[1]) * LOG2E


def pieces_of(full, lane):
    high = full.astype(BF16).astype(F32)
    rest = full - high
    middle = rest.astype(BF16).astype(F32)
    low = rest - middle
    return jnp.where(lane < 32, high, jnp.where(lane < 64, middle, jnp.where(lane < 96, low, 0.0))).astype(BF16)


def partial_kernel(far, start, group, steps, window, kinverse, k, v, kgain, low, high, *refs):
    if far:
        qb, qa, ob, oa = refs[:4]
    else:
        q, qgain, qinverse, part, own_stats = refs[:5]
    kxs, vxs = refs[-2 - 2 * group : -2 - group], refs[-2 - group : -2]
    gaps, st = refs[-2:]
    step = pl.program_id(0)

    @pl.when(step == 0)
    def _():
        for j in range(2):
            st[j, 0] = jnp.zeros((3 * W, HD), F32)
            st[j, 1] = jnp.ones((3 * W, HD), F32)
        fill_ones(vxs)
        fill_gaps(gaps)

    @pl.when(step < steps)
    def _():
        for g in range(group):
            own_keys, own_values = k[:, :, :, lanes(g)], v[:, :, :, lanes(g)]
            fill_lines(
                kxs[g], vxs[g], own_keys, own_values, kinverse[...], kgain[:, lanes(g)], low.at[g], high.at[g]
            )
        if far:
            far_step(start, group, step, window, qb, qa, ob, oa, kxs, vxs, gaps, st)
        else:
            own_step(start, group, step, window, q, qgain, qinverse, part, kxs, vxs, gaps, st)

    if far:

        @pl.when(step == steps)
        def _():
            lane = lax.broadcasted_iota(jnp.int32, (3 * W, HD), 1)
            below, above = (pieces_of(lse_of(st[j]), lane) for j in range(2))
            ob[0], oa[0] = sides("frame", below, above)

    else:

        @pl.when(step == steps - 1)
        def _():
            for j in range(2):
                own_stats[j] = lse_of(st[j])


def marked_lanes(step, group, g):
    return (lax.broadcasted_iota(jnp.int32, (W, HD), 1) & 31) == step * group + g


def far_step(start, group, step, window, qb, qa, ob, oa, kxs, vxs, gaps, st):
    scores = []
    for g in range(group):
        masks = biases(gaps, window, start + step * group + g)
        for i in range(3):
            at = slice(i * W, (i + 1) * W)
            asked = sides("frame", qb[g, at], qa[g, at])
            scores += [dot_t(asked[j], kxs[g][j, lines_of(i)]) + masks[i] for j in range(2)]
    tops = [row_max(s) for s in scores]
    weights = [weights_of(s, top) for s, top in zip(scores, tops)]
    for g in range(group):
        here = marked_lanes(step, group, g)
        for i in range(3):
            at, n = slice(i * W, (i + 1) * W), 6 * g + 2 * i
            mixed = [
                jnp.dot(weights[n + j], vxs[g][j, lines_of(i)], preferred_element_type=F32) for j in range(2)
            ]
            for j in range(2):
                mark(st.at[j], at, here, tops[n + j], mixed[j])
            ob[g, at], oa[g, at] = sides("frame", divided(mixed[0]), divided(mixed[1]))


def own_step(start, group, step, window, q, qgain, qinverse, part, kxs, vxs, gaps, st):
    scores = []
    for g in range(group):
        head = start + step * group + g
        masks = biases(gaps, window, head)
        cross = jnp.where(window[head, 0] > 0, 0.0, NEG)
        qn = normed(q[:, :, :, lanes(g)], qinverse[...], qgain[:, lanes(g)].reshape(1, 1, 1, HD))
        for i in range(3):
            own = qn[:, i].reshape(2 * W, HD)
            other = masks[i] + cross
            for j in range(2):
                raw = dot_t(own, kxs[g][j, lines_of(i)])
                order = (masks[i], other) if j == 0 else (other, masks[i])
                scores.append([raw[W * n : W * (n + 1)] + order[n] for n in range(2)])
    tops, weights = [], []
    for s0, s1 in zip(scores[::2], scores[1::2]):
        top = [row_max(jnp.maximum(s0[n], s1[n])) for n in range(2)]
        tops.append(top)
        for s in (s0, s1):
            weights.append(jnp.concatenate([weights_of(a, b) for a, b in zip(s, top)], axis=0))
    for g in range(group):
        here = marked_lanes(step, group, g)
        for i in range(3):
            at, n = slice(i * W, (i + 1) * W), 3 * g + i
            m0, m1 = (
                jnp.dot(weights[2 * n + j], vxs[g][j, lines_of(i)], preferred_element_type=F32)
                for j in range(2)
            )
            for f in range(2):
                own = m0[W * f : W * (f + 1)] + m1[W * f : W * (f + 1)]
                part[g, f, i] = divided(own)
                mark(st.at[f], at, here, tops[n][f], own)


def partial_call(far, window, k, v, kgain, kinverse, low, high, asked, start, count):
    group = 2
    steps = count // group

    def step_of(s):
        return jnp.minimum(s, steps - 1)

    heads = pl.BlockSpec((2, 3, W, group * HD), lambda s, window: (0, 0, 0, start // group + step_of(s)))
    gains = pl.BlockSpec((1, group * HD), lambda s, window: (0, start // group + step_of(s)))
    rows = pl.BlockSpec((group, 2, 2, W, HD), lambda s, window: (step_of(s), 0, 0, 0, 0))
    norms = whole((2, 3, W, HD))
    if far:
        q_spec = pl.BlockSpec((group, 3 * W, HD), lambda s, window: (step_of(s), 0, 0))
        o_spec = pl.BlockSpec((group, 3 * W, HD), lambda s, window: (s, 0, 0))
        asked_specs, out_specs = [q_spec] * 2, [o_spec] * 2
        out_shape = [jax.ShapeDtypeStruct((count + 1, 3 * W, HD), BF16)] * 2
    else:
        asked_specs = [heads, gains, norms]
        out_specs = [
            pl.BlockSpec((group, 2, 3, W, HD), lambda s, window: (s, 0, 0, 0, 0)),
            whole((2, 3 * W, HD)),
        ]
        out_shape = [
            jax.ShapeDtypeStruct((count, 2, 3, W, HD), BF16),
            jax.ShapeDtypeStruct((2, 3 * W, HD), F32),
        ]
    return pl.pallas_call(
        functools.partial(partial_kernel, far, start, group, steps),
        grid_spec=pltpu.PrefetchScalarGridSpec(
            num_scalar_prefetch=1,
            grid=(steps + 1 if far else steps,),
            in_specs=[norms, heads, heads, gains, rows, rows] + asked_specs,
            out_specs=out_specs,
            scratch_shapes=line_scratch(group)
            + [pltpu.VMEM((2, 3, W, 3 * W), jnp.int32), pltpu.VMEM((2, 2, 3 * W, HD), F32)],
        ),
        out_shape=out_shape,
        compiler_params=params(16),
        cost_estimate=cost(0.6 * count),
        name="far_partial" if far else "own_partial",
    )(window, kinverse, k, v, kgain, low, high, *asked)


def far_partial(window, queries, k, v, kgain, kinverse, rows, start, count):
    return partial_call(True, window, k, v, kgain, kinverse, *rows, queries, start, count)


def own_partial(window, q, k, v, qgain, kgain, qinverse, kinverse, rows, start, count):
    return partial_call(False, window, k, v, kgain, kinverse, *rows, (q, qgain, qinverse), start, count)


def both_kernel(start, group, steps, window, *refs):
    st_own, st_far = refs[-2:]
    ob, oa, own_stats = refs[-6 - 2 * group : -3 - 2 * group]
    step = pl.program_id(0)

    @pl.when(step < steps)
    def _():
        both_step(start, group, step, window, *refs)

    @pl.when(step == steps)
    def _():
        lane = lax.broadcasted_iota(jnp.int32, (3 * W, HD), 1)
        for j in range(2):
            own_stats[j] = lse_of(st_own[j])
        below, above = (pieces_of(lse_of(st_far[j]), lane) for j in range(2))
        ob[0], oa[0] = sides("frame", below, above)


def both_step(start, group, step, window, *refs):
    qinverse, kinverse, qb, qa, q, k, v, qgain, kgain, low, high, part, ob, oa, _ = refs[:15]
    kxs, vxs = refs[15 : 15 + group], refs[15 + group : 15 + 2 * group]
    gaps, st_own, st_far = refs[-3:]
    slot = start + step * group

    @pl.when(step == 0)
    def _():
        for st in (st_own, st_far):
            for j in range(2):
                st[j, 0] = jnp.zeros((3 * W, HD), F32)
                st[j, 1] = jnp.ones((3 * W, HD), F32)
        fill_ones(vxs)
        fill_gaps(gaps)

    scores = []
    for g in range(group):
        own_keys, own_values = k[:, :, :, lanes(g)], v[:, :, :, lanes(g)]
        fill_lines(kxs[g], vxs[g], own_keys, own_values, kinverse[...], kgain[:, lanes(g)], low.at[g], high.at[g])
        masks = biases(gaps, window, slot + g)
        cross = jnp.where(window[slot + g, 0] > 0, 0.0, NEG)
        qn = normed(q[:, :, :, lanes(g)], qinverse[...], qgain[:, lanes(g)].reshape(1, 1, 1, HD))
        for i in range(3):
            own = qn[:, i].reshape(2 * W, HD)
            far = masks[i] + cross
            asked = sides("frame", qb[g, i * W : (i + 1) * W], qa[g, i * W : (i + 1) * W])
            for j in range(2):
                queries = jnp.concatenate([own, asked[j]], axis=0)
                order = [masks[i], far, masks[i]] if j == 0 else [far, masks[i], masks[i]]
                raw = dot_t(queries, kxs[g][j, lines_of(i)])
                scores.append([raw[W * n : W * (n + 1)] + order[n] for n in range(3)])
    tops, weights = [], []
    for s0, s1 in zip(scores[::2], scores[1::2]):
        first, second = (row_max(jnp.maximum(s0[n], s1[n])) for n in range(2))
        below, above = row_max(s0[2]), row_max(s1[2])
        tops.append((jnp.concatenate([first, second], axis=0), below, above))
        for s, last in ((s0, below), (s1, above)):
            parts = [weights_of(a, b) for a, b in zip(s, (first, second, last))]
            weights.append(jnp.concatenate(parts, axis=0))
    lane = lax.broadcasted_iota(jnp.int32, (W, HD), 1)
    for g in range(group):
        here = (lane & 31) == step * group + g
        for i in range(3):
            w0, w1 = weights[6 * g + 2 * i : 6 * g + 2 * i + 2]
            top, top_b, top_a = tops[3 * g + i]
            m0 = jnp.dot(w0, vxs[g][0, lines_of(i)], preferred_element_type=F32)
            m1 = jnp.dot(w1, vxs[g][1, lines_of(i)], preferred_element_type=F32)
            at = slice(i * W, (i + 1) * W)
            for n in range(2):
                own = m0[W * n : W * (n + 1)] + m1[W * n : W * (n + 1)]
                part[g, n, i] = divided(own)
                mark(st_own.at[n], at, here, top[W * n : W * (n + 1)], own)
            for n, far in ((0, m0[2 * W :]), (1, m1[2 * W :])):
                mark(st_far.at[n], at, here, (top_b, top_a)[n], far)
            ob[g, at], oa[g, at] = sides("frame", divided(m0[2 * W :]), divided(m1[2 * W :]))


def both_partial(window, qb, qa, q, k, v, qgain, kgain, qinverse, kinverse, low, high, start, count):
    group = 2
    steps = count // group

    def step_of(s):
        return jnp.minimum(s, steps - 1)

    heads = pl.BlockSpec((2, 3, W, group * HD), lambda s, window: (0, 0, 0, start // group + step_of(s)))
    gains = pl.BlockSpec((1, group * HD), lambda s, window: (0, start // group + step_of(s)))
    rows = pl.BlockSpec((group, 2, 2, W, HD), lambda s, window: (step_of(s), 0, 0, 0, 0))
    q_spec = pl.BlockSpec((group, 3 * W, HD), lambda s, window: (step_of(s), 0, 0))
    o_spec = pl.BlockSpec((group, 3 * W, HD), lambda s, window: (s, 0, 0))
    out = jax.ShapeDtypeStruct((count + 1, 3 * W, HD), BF16)
    stat = pltpu.VMEM((2, 2, 3 * W, HD), F32)
    return pl.pallas_call(
        functools.partial(both_kernel, start, group, steps),
        grid_spec=pltpu.PrefetchScalarGridSpec(
            num_scalar_prefetch=1,
            grid=(steps + 1,),
            in_specs=[whole((2, 3, W, HD))] * 2 + [q_spec] * 2 + [heads] * 3 + [gains] * 2 + [rows] * 2,
            out_specs=[
                pl.BlockSpec((group, 2, 3, W, HD), lambda s, window: (step_of(s), 0, 0, 0, 0)),
                o_spec,
                o_spec,
                whole((2, 3 * W, HD)),
            ],
            scratch_shapes=line_scratch(group) + [pltpu.VMEM((2, 3, W, 3 * W), jnp.int32), stat, stat],
        ),
        out_shape=[
            jax.ShapeDtypeStruct((count, 2, 3, W, HD), BF16),
            out,
            out,
            jax.ShapeDtypeStruct((2, 3 * W, HD), F32),
        ],
        compiler_params=params(16),
        cost_estimate=cost(1.1 * count),
        name="both_partial",
    )(window, qinverse, kinverse, qb, qa, q, k, v, qgain, kgain, low, high)


def merge_kernel(start, group, window, part, lse, ob, oa, sb, sa, *refs):
    out, shares = refs[-2:]
    lane = lax.broadcasted_iota(jnp.int32, (3 * W, HD), 1)
    neighbours = inside("frame")
    step = pl.program_id(0)

    @pl.when(step == 0)
    def _():
        for j, st in enumerate(sides("frame", sb[0], sa[0])):
            pieces = st.astype(F32)
            other = pieces + pltpu.roll(pieces, HD - 32, 1) + pltpu.roll(pieces, HD - 64, 1)
            other = jnp.where(neighbours[j], other, NEG)
            top = jnp.maximum(lse[j], other)
            own_weight = jnp.exp2(lse[j] - top)
            other_weight = jnp.exp2(other - top)
            shares[j] = other_weight / (own_weight + other_weight)

    for g in range(group):
        here = lane == step * group + g
        for j, far in enumerate(sides("frame", ob[g], oa[g])):
            share = jnp.sum(jnp.where(here, shares[j], 0.0), axis=1, keepdims=True)
            share = jnp.where(window[start + step * group + g, 0] > 0, share, 0.0)
            own = part[g, j].reshape(3 * W, HD).astype(F32)
            mixed = own + (far.astype(F32) - own) * share
            out[j, :, :, lanes(g)] = mixed.astype(BF16).reshape(3, W, HD)


def merge(window, out, part, lse, o_below, o_above, start, count):
    group = group_of(start, count)
    o_spec = pl.BlockSpec((group, 3 * W, HD), lambda s, window: (s, 0, 0))
    stat_spec = pl.BlockSpec((1, 3 * W, HD), lambda s, window: (count, 0, 0))
    return pl.pallas_call(
        functools.partial(merge_kernel, start, group),
        grid_spec=pltpu.PrefetchScalarGridSpec(
            num_scalar_prefetch=1,
            grid=(count // group,),
            in_specs=[
                pl.BlockSpec((group, 2, 3, W, HD), lambda s, window: (s, 0, 0, 0, 0)),
                whole((2, 3 * W, HD)),
                o_spec,
                o_spec,
                stat_spec,
                stat_spec,
            ]
            + ([] if out is None else [pl.BlockSpec(memory_space=pl.ANY)]),
            out_specs=heads_spec(start, group),
            scratch_shapes=[pltpu.VMEM((2, 3 * W, HD), F32)],
        ),
        out_shape=jax.ShapeDtypeStruct((2, 3, W, NH * HD), BF16),
        input_output_aliases={} if out is None else {7: 0},
        compiler_params=params(),
        cost_estimate=cost(0.25 * count),
        name="merge",
    )(window, part, lse, o_below, o_above, o_below, o_above, *([] if out is None else [out]))


def exchange(axis, first, second):
    out = []
    for start, block in enumerate((first, second)):
        pairs = [(i, i + 1) for i in range(start, lax.axis_size(axis) - 1, 2)]
        out.append(lax.ppermute(block, axis, pairs + [(b, a) for a, b in pairs]))
    return out


def attention(window, q, k, v, q_gain, k_gain, q_inverse, k_inverse):
    norms = (q_gain, k_gain, q_inverse, k_inverse)
    chunks = ((0, FIRST), (FIRST, NH - FIRST))
    queries, rows = [], []
    for start, count in chunks:
        packed_rows = pack_rows(window, k, v, k_gain, k_inverse, start, count)
        q, *packed_rows = lax.optimization_barrier((q, *packed_rows))
        packed = pack_queries(window, q, q_gain, q_inverse, start, count)
        k, *packed = lax.optimization_barrier((k, *packed))
        if rows:
            packed_rows, packed, rows[0], queries[0] = lax.optimization_barrier(
                (packed_rows, packed, rows[0], queries[0])
            )
        rows.append(exchange("height", *packed_rows))
        queries.append(exchange("frame", *packed))
    (start, count), (late_start, late_count) = chunks
    part, *far, lse = both_partial(window, *queries[0], q, k, v, *norms, *rows[0], start, count)
    parts = [(part, lse, *exchange("frame", *far), start, count)]
    far = far_partial(window, queries[1], k, v, k_gain, k_inverse, rows[1], late_start, late_count)
    part, lse = own_partial(window, q, k, v, *norms, rows[1], late_start, late_count)
    parts.append((part, lse, *exchange("frame", *far), late_start, late_count))
    window, part = lax.optimization_barrier((window, part))
    out = None
    for part in parts:
        out = merge(window, out, *part)
    return out


def squares_of(raw):
    values = raw.astype(F32)
    return jnp.sum(values * values, axis=-1)


def body(q, k, v, q_gain, k_gain, window):
    width_total = q.shape[3] * lax.axis_size("head")
    query_sum, key_sum = lax.psum((squares_of(q), squares_of(k)), "head")

    def inverse_of(total):
        return jnp.broadcast_to(lax.rsqrt(total / width_total + EPS)[..., None], (2, 3, W, HD))

    return attention(
        window, q, k, v, q_gain[None], k_gain[None], inverse_of(query_sum), inverse_of(key_sum)
    )


def solution(mesh):
    placed = (
        P("frame", "height", None, "head"),
        P("frame", "height", None, "head"),
        P("frame", "height", None, "head"),
        P("head"),
        P("head"),
        P("head", None),
    )
    return jax.shard_map(
        body,
        mesh=mesh,
        in_specs=placed,
        out_specs=P("frame", "height", None, "head"),
        check_vma=False,
    )
```

```python
import functools
import math

import jax
import jax.numpy as jnp
from jax import lax
from jax.experimental import pallas as pl
from jax.experimental.pallas import tpu as pltpu
from jax.sharding import PartitionSpec as P

HD = 128
W = 80
NH = 20
FIRST = 10
PIECE = 10
EPS = 1e-06
NEG = -1e30
FAR = 100
LOG2E = math.log2(math.e)
SCALE2 = LOG2E / math.sqrt(HD)
F32 = jnp.float32
BF16 = jnp.bfloat16


def params(mib=12):
    return pltpu.CompilerParams(vmem_limit_bytes=mib * 1024 * 1024)


def cost(microseconds):
    return pl.CostEstimate(flops=0, bytes_accessed=int(microseconds * 3_000_000), transcendentals=0)


def normed(raw, inverse, gain):
    return (raw.astype(F32) * inverse * gain).astype(BF16)


def lanes(g):
    return slice(g * HD, (g + 1) * HD)


def heads_spec(start, group):
    return pl.BlockSpec((2, 3, W, group * HD), lambda s, window: (0, 0, 0, start // group + s))


def gains_spec(start, group):
    return pl.BlockSpec((1, group * HD), lambda s, window: (0, start // group + s))


def whole(shape):
    return pl.BlockSpec(shape, lambda s, window: (0,) * len(shape))


def pack_queries_kernel(group, window, raw, gain, inverse, first, second):
    for g in range(group):
        q = normed(raw[:, :, :, lanes(g)], inverse[...], gain[:, lanes(g)].reshape(1, 1, 1, HD))
        first[g], second[g] = sides("frame", q[0].reshape(3 * W, HD), q[1].reshape(3 * W, HD))


def pack_rows_kernel(group, window, keys, values, gain, inverse, first, second):
    for g in range(group):
        k_gain = gain[:, lanes(g)].reshape(1, 1, HD)
        for n, row_of in (
            (0, lambda row: normed(keys[:, row, :, lanes(g)], inverse[:, row], k_gain)),
            (1, lambda row: values[:, row, :, lanes(g)]),
        ):
            first[g, n], second[g, n] = sides("height", row_of(0), row_of(2))


def group_of(start, count):
    return max(n for n in (1, 2, 4, 5) if count % n == 0 and start % n == 0)


def pack_queries(window, q, gain, inverse, start, count):
    group = group_of(start, count)
    out = jax.ShapeDtypeStruct((count, 3 * W, HD), BF16)
    out_spec = pl.BlockSpec((group, 3 * W, HD), lambda s, window: (s, 0, 0))
    return pl.pallas_call(
        functools.partial(pack_queries_kernel, group),
        grid_spec=pltpu.PrefetchScalarGridSpec(
            num_scalar_prefetch=1,
            grid=(count // group,),
            in_specs=[heads_spec(start, group), gains_spec(start, group), whole((2, 3, W, HD))],
            out_specs=[out_spec, out_spec],
        ),
        out_shape=[out, out],
        compiler_params=params(),
        cost_estimate=cost(0.1 * count),
        name="pack_queries",
    )(window, q, gain, inverse)


def pack_rows(window, k, v, gain, inverse, start, count):
    group = group_of(start, count)
    out = jax.ShapeDtypeStruct((count, 2, 2, W, HD), BF16)
    out_spec = pl.BlockSpec((group, 2, 2, W, HD), lambda s, window: (s, 0, 0, 0, 0))
    return pl.pallas_call(
        functools.partial(pack_rows_kernel, group),
        grid_spec=pltpu.PrefetchScalarGridSpec(
            num_scalar_prefetch=1,
            grid=(count // group,),
            in_specs=[heads_spec(start, group)] * 2 + [gains_spec(start, group), whole((2, 3, W, HD))],
            out_specs=[out_spec, out_spec],
        ),
        out_shape=[out, out],
        compiler_params=params(),
        cost_estimate=cost(0.15 * count),
        name="pack_rows",
    )(window, k, v, gain, inverse)


def fill_lines(kx, vx, k, v, inverse, gain, first, second):
    kn = normed(k, inverse, gain.reshape(1, 1, 1, HD))
    low, high = sides("height", first[...], second[...])
    for j in range(2):
        kx[j, 0:W] = low[0, j]
        kx[j, W : 4 * W] = kn[j].reshape(3 * W, HD)
        kx[j, 4 * W : 5 * W] = high[0, j]
        vx[j, 0:W, 0:HD] = low[1, j]
        vx[j, W : 4 * W, 0:HD] = v[j].reshape(3 * W, HD)
        vx[j, 4 * W : 5 * W, 0:HD] = high[1, j]


def line_scratch(group):
    return [pltpu.VMEM((2, 5 * W, HD), BF16)] * group + [pltpu.VMEM((2, 5 * W, 2 * HD), BF16)] * group


def even(axis):
    return lax.rem(lax.axis_index(axis), 2) == 0


def sides(axis, first, second):
    return jnp.where(even(axis), second, first), jnp.where(even(axis), first, second)


def inside(axis):
    at = lax.axis_index(axis)
    return at > 0, at < lax.axis_size(axis) - 1


def fill_ones(values):
    for vx in values:
        vx[:, :, HD:] = jnp.ones((2, 5 * W, HD), BF16)


def fill_gaps(gaps):
    lane = lax.broadcasted_iota(jnp.int32, (W, 3 * W), 1)
    line = (lane >= W).astype(jnp.int32) + (lane >= 2 * W).astype(jnp.int32)
    key_tile = (lane - W * line) >> 3
    query_tile = lax.broadcasted_iota(jnp.int32, (W, 3 * W), 0) >> 3
    gap = jnp.abs(key_tile - query_tile)
    below, above = inside("height")
    no_low = jnp.where(below, 0, FAR)
    no_high = jnp.where(above, 0, FAR)
    for reach in range(2):
        for i in range(3):
            low = FAR if reach == 0 else (no_low if i == 0 else 0)
            high = FAR if reach == 0 else (no_high if i == 2 else 0)
            gaps[reach, i] = gap + jnp.where(line == 0, low, 0) + jnp.where(line == 2, high, 0)


def biases(gaps, window, head):
    reach_row, reach_tile = jnp.minimum(window[head, 1], 1), window[head, 2]
    return [jnp.where(gaps[reach_row, i] <= reach_tile, 0.0, NEG).astype(F32) for i in range(3)]


def dot_t(q, k):
    return lax.dot_general(q, k, (((1,), (1,)), ((), ())), preferred_element_type=F32)


def lines_of(i):
    return slice(i * W, (i + 3) * W)


def row_max(s):
    return jnp.max(s, axis=-1, keepdims=True)


def weights_of(s, top):
    return jnp.exp2((s - top) * SCALE2).astype(BF16)


def divided(mixed):
    total = mixed[:, HD:]
    inverse = pl.reciprocal(total, approx=True)
    inverse = inverse * (2.0 - total * inverse)
    return (mixed[:, :HD] * inverse).astype(BF16)


def mark(st, at, here, top, mixed):
    st[0, at] = jnp.where(here, top, st[0, at])
    st[1, at] = jnp.where(here, mixed[:, HD:], st[1, at])


def lse_of(st):
    return st[0] * SCALE2 + jnp.log(st[1]) * LOG2E


def pieces_of(full):
    lane = lax.broadcasted_iota(jnp.int32, (3 * W, HD), 1)
    high = full.astype(BF16).astype(F32)
    rest = full - high
    middle = rest.astype(BF16).astype(F32)
    within = lane & 31
    pieces = jnp.where(within < PIECE, high, jnp.where(within < 2 * PIECE, middle, rest - middle))
    lane = lane[:W]
    folded = jnp.where(lane < 32, pieces[:W], jnp.where(lane < 64, pieces[W : 2 * W], pieces[2 * W :]))
    return folded.astype(BF16)


def joined(pieces):
    lines = pieces.astype(F32)
    lines = jnp.concatenate([lines, pltpu.roll(lines, HD - 32, 1), pltpu.roll(lines, HD - 64, 1)], axis=0)
    return lines + pltpu.roll(lines, HD - PIECE, 1) + pltpu.roll(lines, HD - 2 * PIECE, 1)


def partial_kernel(far, start, group, steps, window, kinverse, k, v, kgain, low, high, *refs):
    if far:
        qb, qa, ob, oa = refs[:4]
    else:
        q, qgain, qinverse, part, own_stats = refs[:5]
    kxs, vxs = refs[-2 - 2 * group : -2 - group], refs[-2 - group : -2]
    gaps, st = refs[-2:]
    step = pl.program_id(0)

    @pl.when(step == 0)
    def _():
        for j in range(2):
            st[j, 0] = jnp.zeros((3 * W, HD), F32)
            st[j, 1] = jnp.ones((3 * W, HD), F32)
        fill_ones(vxs)
        fill_gaps(gaps)

    @pl.when(step < steps)
    def _():
        for g in range(group):
            own_keys, own_values = k[:, :, :, lanes(g)], v[:, :, :, lanes(g)]
            fill_lines(
                kxs[g], vxs[g], own_keys, own_values, kinverse[...], kgain[:, lanes(g)], low.at[g], high.at[g]
            )
        if far:
            far_step(start, group, step, window, qb, qa, ob, oa, kxs, vxs, gaps, st)
        else:
            own_step(start, group, step, window, q, qgain, qinverse, part, kxs, vxs, gaps, st)

    if far:

        @pl.when(step == steps)
        def _():
            below, above = (pieces_of(lse_of(st[j])) for j in range(2))
            ob[0], oa[0] = sides("frame", below, above)

    else:

        @pl.when(step == steps - 1)
        def _():
            for j in range(2):
                own_stats[j] = lse_of(st[j])


def marked_lanes(step, group, g):
    within = lax.broadcasted_iota(jnp.int32, (W, HD), 1) & 31
    slot = step * group + g
    return (within == slot) | (within == slot + PIECE) | (within == slot + 2 * PIECE)


def far_step(start, group, step, window, qb, qa, ob, oa, kxs, vxs, gaps, st):
    scores = []
    for g in range(group):
        masks = biases(gaps, window, start + step * group + g)
        for i in range(3):
            at = slice(i * W, (i + 1) * W)
            asked = sides("frame", qb[g, at], qa[g, at])
            scores += [dot_t(asked[j], kxs[g][j, lines_of(i)]) + masks[i] for j in range(2)]
    tops = [row_max(s) for s in scores]
    weights = [weights_of(s, top) for s, top in zip(scores, tops)]
    for g in range(group):
        here = marked_lanes(step, group, g)
        for i in range(3):
            at, n = slice(i * W, (i + 1) * W), 6 * g + 2 * i
            mixed = [
                jnp.dot(weights[n + j], vxs[g][j, lines_of(i)], preferred_element_type=F32) for j in range(2)
            ]
            for j in range(2):
                mark(st.at[j], at, here, tops[n + j], mixed[j])
            ob[3 * g + i], oa[3 * g + i] = sides("frame", divided(mixed[0]), divided(mixed[1]))


def own_step(start, group, step, window, q, qgain, qinverse, part, kxs, vxs, gaps, st):
    scores = []
    for g in range(group):
        head = start + step * group + g
        masks = biases(gaps, window, head)
        cross = jnp.where(window[head, 0] > 0, 0.0, NEG)
        qn = normed(q[:, :, :, lanes(g)], qinverse[...], qgain[:, lanes(g)].reshape(1, 1, 1, HD))
        for i in range(3):
            own = qn[:, i].reshape(2 * W, HD)
            other = masks[i] + cross
            for j in range(2):
                raw = dot_t(own, kxs[g][j, lines_of(i)])
                order = (masks[i], other) if j == 0 else (other, masks[i])
                scores.append([raw[W * n : W * (n + 1)] + order[n] for n in range(2)])
    tops, weights = [], []
    for s0, s1 in zip(scores[::2], scores[1::2]):
        top = [row_max(jnp.maximum(s0[n], s1[n])) for n in range(2)]
        tops.append(top)
        for s in (s0, s1):
            weights.append(jnp.concatenate([weights_of(a, b) for a, b in zip(s, top)], axis=0))
    for g in range(group):
        here = marked_lanes(step, group, g)
        for i in range(3):
            at, n = slice(i * W, (i + 1) * W), 3 * g + i
            m0, m1 = (
                jnp.dot(weights[2 * n + j], vxs[g][j, lines_of(i)], preferred_element_type=F32)
                for j in range(2)
            )
            for f in range(2):
                own = m0[W * f : W * (f + 1)] + m1[W * f : W * (f + 1)]
                part[g, f, i] = divided(own)
                mark(st.at[f], at, here, tops[n][f], own)


def partial_call(far, window, k, v, kgain, kinverse, low, high, asked, start, count):
    group = 2
    steps = count // group

    def step_of(s):
        return jnp.minimum(s, steps - 1)

    heads = pl.BlockSpec((2, 3, W, group * HD), lambda s, window: (0, 0, 0, start // group + step_of(s)))
    gains = pl.BlockSpec((1, group * HD), lambda s, window: (0, start // group + step_of(s)))
    rows = pl.BlockSpec((group, 2, 2, W, HD), lambda s, window: (step_of(s), 0, 0, 0, 0))
    norms = whole((2, 3, W, HD))
    if far:
        q_spec = pl.BlockSpec((group, 3 * W, HD), lambda s, window: (step_of(s), 0, 0))
        o_spec = pl.BlockSpec((3 * group, W, HD), lambda s, window: (s, 0, 0))
        asked_specs, out_specs = [q_spec] * 2, [o_spec] * 2
        out_shape = [jax.ShapeDtypeStruct((3 * count + 1, W, HD), BF16)] * 2
    else:
        asked_specs = [heads, gains, norms]
        out_specs = [
            pl.BlockSpec((group, 2, 3, W, HD), lambda s, window: (s, 0, 0, 0, 0)),
            whole((2, 3 * W, HD)),
        ]
        out_shape = [
            jax.ShapeDtypeStruct((count, 2, 3, W, HD), BF16),
            jax.ShapeDtypeStruct((2, 3 * W, HD), F32),
        ]
    return pl.pallas_call(
        functools.partial(partial_kernel, far, start, group, steps),
        grid_spec=pltpu.PrefetchScalarGridSpec(
            num_scalar_prefetch=1,
            grid=(steps + 1 if far else steps,),
            in_specs=[norms, heads, heads, gains, rows, rows] + asked_specs,
            out_specs=out_specs,
            scratch_shapes=line_scratch(group)
            + [pltpu.VMEM((2, 3, W, 3 * W), jnp.int32), pltpu.VMEM((2, 2, 3 * W, HD), F32)],
        ),
        out_shape=out_shape,
        compiler_params=params(16),
        cost_estimate=cost(0.6 * count),
        name="far_partial" if far else "own_partial",
    )(window, kinverse, k, v, kgain, low, high, *asked)


def far_partial(window, queries, k, v, kgain, kinverse, rows, start, count):
    return partial_call(True, window, k, v, kgain, kinverse, *rows, queries, start, count)


def own_partial(window, q, k, v, qgain, kgain, qinverse, kinverse, rows, start, count):
    return partial_call(False, window, k, v, kgain, kinverse, *rows, (q, qgain, qinverse), start, count)


def both_kernel(start, group, steps, window, *refs):
    st_own, st_far = refs[-2:]
    ob, oa, own_stats = refs[-6 - 2 * group : -3 - 2 * group]
    step = pl.program_id(0)

    @pl.when(step < steps)
    def _():
        both_step(start, group, step, window, *refs)

    @pl.when(step == steps)
    def _():
        for j in range(2):
            own_stats[j] = lse_of(st_own[j])
        below, above = (pieces_of(lse_of(st_far[j])) for j in range(2))
        ob[0], oa[0] = sides("frame", below, above)


def both_step(start, group, step, window, *refs):
    qinverse, kinverse, qb, qa, q, k, v, qgain, kgain, low, high, part, ob, oa, _ = refs[:15]
    kxs, vxs = refs[15 : 15 + group], refs[15 + group : 15 + 2 * group]
    gaps, st_own, st_far = refs[-3:]
    slot = start + step * group

    @pl.when(step == 0)
    def _():
        for st in (st_own, st_far):
            for j in range(2):
                st[j, 0] = jnp.zeros((3 * W, HD), F32)
                st[j, 1] = jnp.ones((3 * W, HD), F32)
        fill_ones(vxs)
        fill_gaps(gaps)

    scores = []
    for g in range(group):
        own_keys, own_values = k[:, :, :, lanes(g)], v[:, :, :, lanes(g)]
        fill_lines(kxs[g], vxs[g], own_keys, own_values, kinverse[...], kgain[:, lanes(g)], low.at[g], high.at[g])
        masks = biases(gaps, window, slot + g)
        cross = jnp.where(window[slot + g, 0] > 0, 0.0, NEG)
        qn = normed(q[:, :, :, lanes(g)], qinverse[...], qgain[:, lanes(g)].reshape(1, 1, 1, HD))
        for i in range(3):
            own = qn[:, i].reshape(2 * W, HD)
            far = masks[i] + cross
            asked = sides("frame", qb[g, i * W : (i + 1) * W], qa[g, i * W : (i + 1) * W])
            for j in range(2):
                queries = jnp.concatenate([own, asked[j]], axis=0)
                order = [masks[i], far, masks[i]] if j == 0 else [far, masks[i], masks[i]]
                raw = dot_t(queries, kxs[g][j, lines_of(i)])
                scores.append([raw[W * n : W * (n + 1)] + order[n] for n in range(3)])
    tops, weights = [], []
    for s0, s1 in zip(scores[::2], scores[1::2]):
        first, second = (row_max(jnp.maximum(s0[n], s1[n])) for n in range(2))
        below, above = row_max(s0[2]), row_max(s1[2])
        tops.append((jnp.concatenate([first, second], axis=0), below, above))
        for s, last in ((s0, below), (s1, above)):
            parts = [weights_of(a, b) for a, b in zip(s, (first, second, last))]
            weights.append(jnp.concatenate(parts, axis=0))
    for g in range(group):
        here = marked_lanes(step, group, g)
        for i in range(3):
            w0, w1 = weights[6 * g + 2 * i : 6 * g + 2 * i + 2]
            top, top_b, top_a = tops[3 * g + i]
            m0 = jnp.dot(w0, vxs[g][0, lines_of(i)], preferred_element_type=F32)
            m1 = jnp.dot(w1, vxs[g][1, lines_of(i)], preferred_element_type=F32)
            at = slice(i * W, (i + 1) * W)
            for n in range(2):
                own = m0[W * n : W * (n + 1)] + m1[W * n : W * (n + 1)]
                part[g, n, i] = divided(own)
                mark(st_own.at[n], at, here, top[W * n : W * (n + 1)], own)
            for n, far in ((0, m0[2 * W :]), (1, m1[2 * W :])):
                mark(st_far.at[n], at, here, (top_b, top_a)[n], far)
            ob[3 * g + i], oa[3 * g + i] = sides("frame", divided(m0[2 * W :]), divided(m1[2 * W :]))


def both_partial(window, qb, qa, q, k, v, qgain, kgain, qinverse, kinverse, low, high, start, count):
    group = 2
    steps = count // group

    def step_of(s):
        return jnp.minimum(s, steps - 1)

    heads = pl.BlockSpec((2, 3, W, group * HD), lambda s, window: (0, 0, 0, start // group + step_of(s)))
    gains = pl.BlockSpec((1, group * HD), lambda s, window: (0, start // group + step_of(s)))
    rows = pl.BlockSpec((group, 2, 2, W, HD), lambda s, window: (step_of(s), 0, 0, 0, 0))
    q_spec = pl.BlockSpec((group, 3 * W, HD), lambda s, window: (step_of(s), 0, 0))
    o_spec = pl.BlockSpec((3 * group, W, HD), lambda s, window: (s, 0, 0))
    out = jax.ShapeDtypeStruct((3 * count + 1, W, HD), BF16)
    stat = pltpu.VMEM((2, 2, 3 * W, HD), F32)
    return pl.pallas_call(
        functools.partial(both_kernel, start, group, steps),
        grid_spec=pltpu.PrefetchScalarGridSpec(
            num_scalar_prefetch=1,
            grid=(steps + 1,),
            in_specs=[whole((2, 3, W, HD))] * 2 + [q_spec] * 2 + [heads] * 3 + [gains] * 2 + [rows] * 2,
            out_specs=[
                pl.BlockSpec((group, 2, 3, W, HD), lambda s, window: (step_of(s), 0, 0, 0, 0)),
                o_spec,
                o_spec,
                whole((2, 3 * W, HD)),
            ],
            scratch_shapes=line_scratch(group) + [pltpu.VMEM((2, 3, W, 3 * W), jnp.int32), stat, stat],
        ),
        out_shape=[
            jax.ShapeDtypeStruct((count, 2, 3, W, HD), BF16),
            out,
            out,
            jax.ShapeDtypeStruct((2, 3 * W, HD), F32),
        ],
        compiler_params=params(16),
        cost_estimate=cost(1.1 * count),
        name="both_partial",
    )(window, qinverse, kinverse, qb, qa, q, k, v, qgain, kgain, low, high)


def merge_kernel(start, group, window, part, lse, ob, oa, sb, sa, *refs):
    out, shares = refs[-2:]
    lane = lax.broadcasted_iota(jnp.int32, (3 * W, HD), 1)
    neighbours = inside("frame")
    step = pl.program_id(0)

    @pl.when(step == 0)
    def _():
        for j, st in enumerate(sides("frame", sb[0], sa[0])):
            other = jnp.where(neighbours[j], joined(st), NEG)
            top = jnp.maximum(lse[j], other)
            own_weight = jnp.exp2(lse[j] - top)
            other_weight = jnp.exp2(other - top)
            shares[j] = other_weight / (own_weight + other_weight)

    for g in range(group):
        here = lane == step * group + g
        for j, far in enumerate(sides("frame", ob[3 * g : 3 * g + 3], oa[3 * g : 3 * g + 3])):
            share = jnp.sum(jnp.where(here, shares[j], 0.0), axis=1, keepdims=True)
            share = jnp.where(window[start + step * group + g, 0] > 0, share, 0.0)
            own = part[g, j].reshape(3 * W, HD).astype(F32)
            mixed = own + (far.reshape(3 * W, HD).astype(F32) - own) * share
            out[j, :, :, lanes(g)] = mixed.astype(BF16).reshape(3, W, HD)


def merge(window, out, part, lse, o_below, o_above, start, count):
    group = group_of(start, count)
    o_spec = pl.BlockSpec((3 * group, W, HD), lambda s, window: (s, 0, 0))
    stat_spec = pl.BlockSpec((1, W, HD), lambda s, window: (3 * count, 0, 0))
    return pl.pallas_call(
        functools.partial(merge_kernel, start, group),
        grid_spec=pltpu.PrefetchScalarGridSpec(
            num_scalar_prefetch=1,
            grid=(count // group,),
            in_specs=[
                pl.BlockSpec((group, 2, 3, W, HD), lambda s, window: (s, 0, 0, 0, 0)),
                whole((2, 3 * W, HD)),
                o_spec,
                o_spec,
                stat_spec,
                stat_spec,
            ]
            + ([] if out is None else [pl.BlockSpec(memory_space=pl.ANY)]),
            out_specs=heads_spec(start, group),
            scratch_shapes=[pltpu.VMEM((2, 3 * W, HD), F32)],
        ),
        out_shape=jax.ShapeDtypeStruct((2, 3, W, NH * HD), BF16),
        input_output_aliases={} if out is None else {7: 0},
        compiler_params=params(),
        cost_estimate=cost(0.25 * count),
        name="merge",
    )(window, part, lse, o_below, o_above, o_below, o_above, *([] if out is None else [out]))


def exchange(axis, first, second):
    out = []
    for start, block in enumerate((first, second)):
        pairs = [(i, i + 1) for i in range(start, lax.axis_size(axis) - 1, 2)]
        out.append(lax.ppermute(block, axis, pairs + [(b, a) for a, b in pairs]))
    return out


def attention(window, q, k, v, q_gain, k_gain, q_inverse, k_inverse):
    norms = (q_gain, k_gain, q_inverse, k_inverse)
    chunks = ((0, FIRST), (FIRST, NH - FIRST))
    queries, rows = [], []
    for start, count in chunks:
        packed = pack_queries(window, q, q_gain, q_inverse, start, count)
        k, *packed = lax.optimization_barrier((k, *packed))
        packed_rows = pack_rows(window, k, v, k_gain, k_inverse, start, count)
        rows.append(exchange("height", *packed_rows))
        queries.append(exchange("frame", *packed))
        q, *_ = lax.optimization_barrier((q, *packed_rows))
    (start, count), (late_start, late_count) = chunks
    part, *far, lse = both_partial(window, *queries[0], q, k, v, *norms, *rows[0], start, count)
    parts = [(part, lse, *exchange("frame", *far), start, count)]
    far = far_partial(window, queries[1], k, v, k_gain, k_inverse, rows[1], late_start, late_count)
    part, lse = own_partial(window, q, k, v, *norms, rows[1], late_start, late_count)
    parts.append((part, lse, *exchange("frame", *far), late_start, late_count))
    out = None
    for part in parts:
        out = merge(window, out, *part)
    return out


def squares_of(raw):
    values = raw.astype(F32)
    return jnp.sum(values * values, axis=-1)


def body(q, k, v, q_gain, k_gain, window):
    width_total = q.shape[3] * lax.axis_size("head")
    query_sum, key_sum = lax.psum((squares_of(q), squares_of(k)), "head")

    def inverse_of(total):
        return jnp.broadcast_to(lax.rsqrt(total / width_total + EPS)[..., None], (2, 3, W, HD))

    return attention(
        window, q, k, v, q_gain[None], k_gain[None], inverse_of(query_sum), inverse_of(key_sum)
    )


def solution(mesh):
    placed = (
        P("frame", "height", None, "head"),
        P("frame", "height", None, "head"),
        P("frame", "height", None, "head"),
        P("head"),
        P("head"),
        P("head", None),
    )
    return jax.shard_map(
        body,
        mesh=mesh,
        in_specs=placed,
        out_specs=P("frame", "height", None, "head"),
        check_vma=False,
    )
```

```python
import functools
import math

import jax
import jax.numpy as jnp
from jax import lax
from jax.experimental import pallas as pl
from jax.experimental.pallas import tpu as pltpu
from jax.sharding import PartitionSpec as P

HD = 128
W = 80
NH = 20
FIRST = 10
PIECE = 10
EPS = 1e-06
NEG = -1e30
FAR = 100
LOG2E = math.log2(math.e)
SCALE2 = LOG2E / math.sqrt(HD)
F32 = jnp.float32
BF16 = jnp.bfloat16


def params(mib=12):
    return pltpu.CompilerParams(vmem_limit_bytes=mib * 1024 * 1024)


def cost(microseconds):
    return pl.CostEstimate(flops=0, bytes_accessed=int(microseconds * 3_000_000), transcendentals=0)


def normed(raw, inverse, gain):
    return (raw.astype(F32) * inverse * gain).astype(BF16)


def lanes(g):
    return slice(g * HD, (g + 1) * HD)


def heads_spec(start, group):
    return pl.BlockSpec((2, 3, W, group * HD), lambda s, window: (0, 0, 0, start // group + s))


def gains_spec(start, group):
    return pl.BlockSpec((1, group * HD), lambda s, window: (0, start // group + s))


def whole(shape):
    return pl.BlockSpec(shape, lambda s, window: (0,) * len(shape))


def pack_queries_kernel(group, window, raw, gain, inverse, first, second):
    for g in range(group):
        q = normed(raw[:, :, :, lanes(g)], inverse[...], gain[:, lanes(g)].reshape(1, 1, 1, HD))
        first[g], second[g] = sides("frame", q[0].reshape(3 * W, HD), q[1].reshape(3 * W, HD))


def pack_rows_kernel(group, window, keys, values, gain, inverse, first, second):
    for g in range(group):
        k_gain = gain[:, lanes(g)].reshape(1, 1, HD)
        for n, row_of in (
            (0, lambda row: normed(keys[:, row, :, lanes(g)], inverse[:, row], k_gain)),
            (1, lambda row: values[:, row, :, lanes(g)]),
        ):
            first[g, n], second[g, n] = sides("height", row_of(0), row_of(2))


def group_of(start, count):
    return max(n for n in (1, 2, 4, 5) if count % n == 0 and start % n == 0)


def pack_queries(window, q, gain, inverse, start, count):
    group = group_of(start, count)
    out = jax.ShapeDtypeStruct((count, 3 * W, HD), BF16)
    out_spec = pl.BlockSpec((group, 3 * W, HD), lambda s, window: (s, 0, 0))
    return pl.pallas_call(
        functools.partial(pack_queries_kernel, group),
        grid_spec=pltpu.PrefetchScalarGridSpec(
            num_scalar_prefetch=1,
            grid=(count // group,),
            in_specs=[heads_spec(start, group), gains_spec(start, group), whole((2, 3, W, HD))],
            out_specs=[out_spec, out_spec],
        ),
        out_shape=[out, out],
        compiler_params=params(),
        cost_estimate=cost(0.1 * count),
        name="pack_queries",
    )(window, q, gain, inverse)


def pack_rows(window, k, v, gain, inverse, start, count):
    group = group_of(start, count)
    out = jax.ShapeDtypeStruct((count, 2, 2, W, HD), BF16)
    out_spec = pl.BlockSpec((group, 2, 2, W, HD), lambda s, window: (s, 0, 0, 0, 0))
    return pl.pallas_call(
        functools.partial(pack_rows_kernel, group),
        grid_spec=pltpu.PrefetchScalarGridSpec(
            num_scalar_prefetch=1,
            grid=(count // group,),
            in_specs=[heads_spec(start, group)] * 2 + [gains_spec(start, group), whole((2, 3, W, HD))],
            out_specs=[out_spec, out_spec],
        ),
        out_shape=[out, out],
        compiler_params=params(),
        cost_estimate=cost(0.15 * count),
        name="pack_rows",
    )(window, k, v, gain, inverse)


def fill_lines(kx, vx, k, v, inverse, gain, first, second):
    kn = normed(k, inverse, gain.reshape(1, 1, 1, HD))
    low, high = sides("height", first[...], second[...])
    for j in range(2):
        kx[j, 0:W] = low[0, j]
        kx[j, W : 4 * W] = kn[j].reshape(3 * W, HD)
        kx[j, 4 * W : 5 * W] = high[0, j]
        vx[j, 0:W, 0:HD] = low[1, j]
        vx[j, W : 4 * W, 0:HD] = v[j].reshape(3 * W, HD)
        vx[j, 4 * W : 5 * W, 0:HD] = high[1, j]


def line_scratch(group):
    return [pltpu.VMEM((2, 5 * W, HD), BF16)] * group + [pltpu.VMEM((2, 5 * W, 2 * HD), BF16)] * group


def even(axis):
    return lax.rem(lax.axis_index(axis), 2) == 0


def sides(axis, first, second):
    return jnp.where(even(axis), second, first), jnp.where(even(axis), first, second)


def inside(axis):
    at = lax.axis_index(axis)
    return at > 0, at < lax.axis_size(axis) - 1


def fill_ones(values):
    for vx in values:
        vx[:, :, HD:] = jnp.ones((2, 5 * W, HD), BF16)


def fill_gaps(gaps):
    lane = lax.broadcasted_iota(jnp.int32, (W, 3 * W), 1)
    line = (lane >= W).astype(jnp.int32) + (lane >= 2 * W).astype(jnp.int32)
    key_tile = (lane - W * line) >> 3
    query_tile = lax.broadcasted_iota(jnp.int32, (W, 3 * W), 0) >> 3
    gap = jnp.abs(key_tile - query_tile)
    below, above = inside("height")
    no_low = jnp.where(below, 0, FAR)
    no_high = jnp.where(above, 0, FAR)
    for reach in range(2):
        for i in range(3):
            low = FAR if reach == 0 else (no_low if i == 0 else 0)
            high = FAR if reach == 0 else (no_high if i == 2 else 0)
            gaps[reach, i] = gap + jnp.where(line == 0, low, 0) + jnp.where(line == 2, high, 0)


def biases(gaps, window, head):
    reach_row, reach_tile = jnp.minimum(window[head, 1], 1), window[head, 2]
    return [jnp.where(gaps[reach_row, i] <= reach_tile, 0.0, NEG).astype(F32) for i in range(3)]


def dot_t(q, k):
    return lax.dot_general(q, k, (((1,), (1,)), ((), ())), preferred_element_type=F32)


def lines_of(i):
    return slice(i * W, (i + 3) * W)


def row_max(s):
    return jnp.max(s, axis=-1, keepdims=True)


def weights_of(s, top):
    return jnp.exp2((s - top) * SCALE2).astype(BF16)


def divided(mixed):
    total = mixed[:, HD:]
    inverse = pl.reciprocal(total, approx=True)
    inverse = inverse * (2.0 - total * inverse)
    return (mixed[:, :HD] * inverse).astype(BF16)


def mark(st, at, here, top, mixed):
    st[0, at] = jnp.where(here, top, st[0, at])
    st[1, at] = jnp.where(here, mixed[:, HD:], st[1, at])


def lse_of(st):
    return st[0] * SCALE2 + jnp.log(st[1]) * LOG2E


def pieces_of(full):
    lane = lax.broadcasted_iota(jnp.int32, (3 * W, HD), 1)
    high = full.astype(BF16).astype(F32)
    rest = full - high
    middle = rest.astype(BF16).astype(F32)
    within = lane & 31
    pieces = jnp.where(within < PIECE, high, jnp.where(within < 2 * PIECE, middle, rest - middle))
    lane = lane[:W]
    folded = jnp.where(lane < 32, pieces[:W], jnp.where(lane < 64, pieces[W : 2 * W], pieces[2 * W :]))
    return folded.astype(BF16)


def joined(pieces):
    lines = pieces.astype(F32)
    lines = jnp.concatenate([lines, pltpu.roll(lines, HD - 32, 1), pltpu.roll(lines, HD - 64, 1)], axis=0)
    return lines + pltpu.roll(lines, HD - PIECE, 1) + pltpu.roll(lines, HD - 2 * PIECE, 1)


def partial_kernel(far, start, group, steps, window, kinverse, k, v, kgain, low, high, *refs):
    if far:
        qb, qa, ob, oa = refs[:4]
    else:
        q, qgain, qinverse, part, own_stats = refs[:5]
    kxs, vxs = refs[-2 - 2 * group : -2 - group], refs[-2 - group : -2]
    gaps, st = refs[-2:]
    step = pl.program_id(0)

    @pl.when(step == 0)
    def _():
        for j in range(2):
            st[j, 0] = jnp.zeros((3 * W, HD), F32)
            st[j, 1] = jnp.ones((3 * W, HD), F32)
        fill_ones(vxs)
        fill_gaps(gaps)

    @pl.when(step < steps)
    def _():
        for g in range(group):
            own_keys, own_values = k[:, :, :, lanes(g)], v[:, :, :, lanes(g)]
            fill_lines(
                kxs[g], vxs[g], own_keys, own_values, kinverse[...], kgain[:, lanes(g)], low.at[g], high.at[g]
            )
        if far:
            far_step(start, group, step, window, qb, qa, ob, oa, kxs, vxs, gaps, st)
        else:
            own_step(start, group, step, window, q, qgain, qinverse, part, kxs, vxs, gaps, st)

    if far:

        @pl.when(step == steps)
        def _():
            below, above = (pieces_of(lse_of(st[j])) for j in range(2))
            ob[0], oa[0] = sides("frame", below, above)

    else:

        @pl.when(step == steps - 1)
        def _():
            for j in range(2):
                own_stats[j] = lse_of(st[j])


def marked_lanes(step, group, g):
    within = lax.broadcasted_iota(jnp.int32, (W, HD), 1) & 31
    slot = step * group + g
    return (within == slot) | (within == slot + PIECE) | (within == slot + 2 * PIECE)


def far_step(start, group, step, window, qb, qa, ob, oa, kxs, vxs, gaps, st):
    scores = []
    for g in range(group):
        masks = biases(gaps, window, start + step * group + g)
        for i in range(3):
            at = slice(i * W, (i + 1) * W)
            asked = sides("frame", qb[g, at], qa[g, at])
            scores += [dot_t(asked[j], kxs[g][j, lines_of(i)]) + masks[i] for j in range(2)]
    tops = [row_max(s) for s in scores]
    weights = [weights_of(s, top) for s, top in zip(scores, tops)]
    for g in range(group):
        here = marked_lanes(step, group, g)
        for i in range(3):
            at, n = slice(i * W, (i + 1) * W), 6 * g + 2 * i
            mixed = [
                jnp.dot(weights[n + j], vxs[g][j, lines_of(i)], preferred_element_type=F32) for j in range(2)
            ]
            for j in range(2):
                mark(st.at[j], at, here, tops[n + j], mixed[j])
            ob[3 * g + i], oa[3 * g + i] = sides("frame", divided(mixed[0]), divided(mixed[1]))


def own_step(start, group, step, window, q, qgain, qinverse, part, kxs, vxs, gaps, st):
    scores = []
    for g in range(group):
        head = start + step * group + g
        masks = biases(gaps, window, head)
        cross = jnp.where(window[head, 0] > 0, 0.0, NEG)
        qn = normed(q[:, :, :, lanes(g)], qinverse[...], qgain[:, lanes(g)].reshape(1, 1, 1, HD))
        for i in range(3):
            own = qn[:, i].reshape(2 * W, HD)
            other = masks[i] + cross
            for j in range(2):
                raw = dot_t(own, kxs[g][j, lines_of(i)])
                order = (masks[i], other) if j == 0 else (other, masks[i])
                scores.append([raw[W * n : W * (n + 1)] + order[n] for n in range(2)])
    tops, weights = [], []
    for s0, s1 in zip(scores[::2], scores[1::2]):
        top = [row_max(jnp.maximum(s0[n], s1[n])) for n in range(2)]
        tops.append(top)
        for s in (s0, s1):
            weights.append(jnp.concatenate([weights_of(a, b) for a, b in zip(s, top)], axis=0))
    for g in range(group):
        here = marked_lanes(step, group, g)
        for i in range(3):
            at, n = slice(i * W, (i + 1) * W), 3 * g + i
            m0, m1 = (
                jnp.dot(weights[2 * n + j], vxs[g][j, lines_of(i)], preferred_element_type=F32)
                for j in range(2)
            )
            for f in range(2):
                own = m0[W * f : W * (f + 1)] + m1[W * f : W * (f + 1)]
                part[g, f, i] = divided(own)
                mark(st.at[f], at, here, tops[n][f], own)


def partial_call(far, window, k, v, kgain, kinverse, low, high, asked, start, count):
    group = 2
    steps = count // group

    def step_of(s):
        return jnp.minimum(s, steps - 1)

    heads = pl.BlockSpec((2, 3, W, group * HD), lambda s, window: (0, 0, 0, start // group + step_of(s)))
    gains = pl.BlockSpec((1, group * HD), lambda s, window: (0, start // group + step_of(s)))
    rows = pl.BlockSpec((group, 2, 2, W, HD), lambda s, window: (step_of(s), 0, 0, 0, 0))
    norms = whole((2, 3, W, HD))
    if far:
        q_spec = pl.BlockSpec((group, 3 * W, HD), lambda s, window: (step_of(s), 0, 0))
        o_spec = pl.BlockSpec((3 * group, W, HD), lambda s, window: (s, 0, 0))
        asked_specs, out_specs = [q_spec] * 2, [o_spec] * 2
        out_shape = [jax.ShapeDtypeStruct((3 * count + 1, W, HD), BF16)] * 2
    else:
        asked_specs = [heads, gains, norms]
        out_specs = [
            pl.BlockSpec((group, 2, 3, W, HD), lambda s, window: (s, 0, 0, 0, 0)),
            whole((2, 3 * W, HD)),
        ]
        out_shape = [
            jax.ShapeDtypeStruct((count, 2, 3, W, HD), BF16),
            jax.ShapeDtypeStruct((2, 3 * W, HD), F32),
        ]
    return pl.pallas_call(
        functools.partial(partial_kernel, far, start, group, steps),
        grid_spec=pltpu.PrefetchScalarGridSpec(
            num_scalar_prefetch=1,
            grid=(steps + 1 if far else steps,),
            in_specs=[norms, heads, heads, gains, rows, rows] + asked_specs,
            out_specs=out_specs,
            scratch_shapes=line_scratch(group)
            + [pltpu.VMEM((2, 3, W, 3 * W), jnp.int32), pltpu.VMEM((2, 2, 3 * W, HD), F32)],
        ),
        out_shape=out_shape,
        compiler_params=params(16),
        cost_estimate=cost(0.6 * count),
        name="far_partial" if far else "own_partial",
    )(window, kinverse, k, v, kgain, low, high, *asked)


def far_partial(window, queries, k, v, kgain, kinverse, rows, start, count):
    return partial_call(True, window, k, v, kgain, kinverse, *rows, queries, start, count)


def own_partial(window, q, k, v, qgain, kgain, qinverse, kinverse, rows, start, count):
    return partial_call(False, window, k, v, kgain, kinverse, *rows, (q, qgain, qinverse), start, count)


def both_kernel(start, group, steps, window, *refs):
    st_own, st_far = refs[-2:]
    ob, oa, own_stats = refs[-6 - 2 * group : -3 - 2 * group]
    step = pl.program_id(0)

    @pl.when(step < steps)
    def _():
        both_step(start, group, step, window, *refs)

    @pl.when(step == steps)
    def _():
        for j in range(2):
            own_stats[j] = lse_of(st_own[j])
        below, above = (pieces_of(lse_of(st_far[j])) for j in range(2))
        ob[0], oa[0] = sides("frame", below, above)


def both_step(start, group, step, window, *refs):
    qinverse, kinverse, qb, qa, q, k, v, qgain, kgain, low, high, part, ob, oa, _ = refs[:15]
    kxs, vxs = refs[15 : 15 + group], refs[15 + group : 15 + 2 * group]
    gaps, st_own, st_far = refs[-3:]
    slot = start + step * group

    @pl.when(step == 0)
    def _():
        for st in (st_own, st_far):
            for j in range(2):
                st[j, 0] = jnp.zeros((3 * W, HD), F32)
                st[j, 1] = jnp.ones((3 * W, HD), F32)
        fill_ones(vxs)
        fill_gaps(gaps)

    scores = []
    for g in range(group):
        own_keys, own_values = k[:, :, :, lanes(g)], v[:, :, :, lanes(g)]
        fill_lines(kxs[g], vxs[g], own_keys, own_values, kinverse[...], kgain[:, lanes(g)], low.at[g], high.at[g])
        masks = biases(gaps, window, slot + g)
        cross = jnp.where(window[slot + g, 0] > 0, 0.0, NEG)
        qn = normed(q[:, :, :, lanes(g)], qinverse[...], qgain[:, lanes(g)].reshape(1, 1, 1, HD))
        for i in range(3):
            own = qn[:, i].reshape(2 * W, HD)
            far = masks[i] + cross
            asked = sides("frame", qb[g, i * W : (i + 1) * W], qa[g, i * W : (i + 1) * W])
            for j in range(2):
                queries = jnp.concatenate([own, asked[j]], axis=0)
                order = [masks[i], far, masks[i]] if j == 0 else [far, masks[i], masks[i]]
                raw = dot_t(queries, kxs[g][j, lines_of(i)])
                scores.append([raw[W * n : W * (n + 1)] + order[n] for n in range(3)])
    tops, weights = [], []
    for s0, s1 in zip(scores[::2], scores[1::2]):
        first, second = (row_max(jnp.maximum(s0[n], s1[n])) for n in range(2))
        below, above = row_max(s0[2]), row_max(s1[2])
        tops.append((jnp.concatenate([first, second], axis=0), below, above))
        for s, last in ((s0, below), (s1, above)):
            parts = [weights_of(a, b) for a, b in zip(s, (first, second, last))]
            weights.append(jnp.concatenate(parts, axis=0))
    for g in range(group):
        here = marked_lanes(step, group, g)
        for i in range(3):
            w0, w1 = weights[6 * g + 2 * i : 6 * g + 2 * i + 2]
            top, top_b, top_a = tops[3 * g + i]
            m0 = jnp.dot(w0, vxs[g][0, lines_of(i)], preferred_element_type=F32)
            m1 = jnp.dot(w1, vxs[g][1, lines_of(i)], preferred_element_type=F32)
            at = slice(i * W, (i + 1) * W)
            for n in range(2):
                own = m0[W * n : W * (n + 1)] + m1[W * n : W * (n + 1)]
                part[g, n, i] = divided(own)
                mark(st_own.at[n], at, here, top[W * n : W * (n + 1)], own)
            for n, far in ((0, m0[2 * W :]), (1, m1[2 * W :])):
                mark(st_far.at[n], at, here, (top_b, top_a)[n], far)
            ob[3 * g + i], oa[3 * g + i] = sides("frame", divided(m0[2 * W :]), divided(m1[2 * W :]))


def both_partial(window, qb, qa, q, k, v, qgain, kgain, qinverse, kinverse, low, high, start, count):
    group = 2
    steps = count // group

    def step_of(s):
        return jnp.minimum(s, steps - 1)

    heads = pl.BlockSpec((2, 3, W, group * HD), lambda s, window: (0, 0, 0, start // group + step_of(s)))
    gains = pl.BlockSpec((1, group * HD), lambda s, window: (0, start // group + step_of(s)))
    rows = pl.BlockSpec((group, 2, 2, W, HD), lambda s, window: (step_of(s), 0, 0, 0, 0))
    q_spec = pl.BlockSpec((group, 3 * W, HD), lambda s, window: (step_of(s), 0, 0))
    o_spec = pl.BlockSpec((3 * group, W, HD), lambda s, window: (s, 0, 0))
    out = jax.ShapeDtypeStruct((3 * count + 1, W, HD), BF16)
    stat = pltpu.VMEM((2, 2, 3 * W, HD), F32)
    return pl.pallas_call(
        functools.partial(both_kernel, start, group, steps),
        grid_spec=pltpu.PrefetchScalarGridSpec(
            num_scalar_prefetch=1,
            grid=(steps + 1,),
            in_specs=[whole((2, 3, W, HD))] * 2 + [q_spec] * 2 + [heads] * 3 + [gains] * 2 + [rows] * 2,
            out_specs=[
                pl.BlockSpec((group, 2, 3, W, HD), lambda s, window: (step_of(s), 0, 0, 0, 0)),
                o_spec,
                o_spec,
                whole((2, 3 * W, HD)),
            ],
            scratch_shapes=line_scratch(group) + [pltpu.VMEM((2, 3, W, 3 * W), jnp.int32), stat, stat],
        ),
        out_shape=[
            jax.ShapeDtypeStruct((count, 2, 3, W, HD), BF16),
            out,
            out,
            jax.ShapeDtypeStruct((2, 3 * W, HD), F32),
        ],
        compiler_params=params(16),
        cost_estimate=cost(1.1 * count),
        name="both_partial",
    )(window, qinverse, kinverse, qb, qa, q, k, v, qgain, kgain, low, high)


def merge_kernel(start, group, window, part, lse, ob, oa, sb, sa, *refs):
    out, shares = refs[-2:]
    lane = lax.broadcasted_iota(jnp.int32, (3 * W, HD), 1)
    neighbours = inside("frame")
    step = pl.program_id(0)

    @pl.when(step == 0)
    def _():
        for j, st in enumerate(sides("frame", sb[0], sa[0])):
            other = jnp.where(neighbours[j], joined(st), NEG)
            top = jnp.maximum(lse[j], other)
            own_weight = jnp.exp2(lse[j] - top)
            other_weight = jnp.exp2(other - top)
            shares[j] = other_weight / (own_weight + other_weight)

    for g in range(group):
        here = lane == step * group + g
        for j, far in enumerate(sides("frame", ob[3 * g : 3 * g + 3], oa[3 * g : 3 * g + 3])):
            share = jnp.sum(jnp.where(here, shares[j], 0.0), axis=1, keepdims=True)
            share = jnp.where(window[start + step * group + g, 0] > 0, share, 0.0)
            own = part[g, j].reshape(3 * W, HD).astype(F32)
            mixed = own + (far.reshape(3 * W, HD).astype(F32) - own) * share
            out[j, :, :, lanes(g)] = mixed.astype(BF16).reshape(3, W, HD)


def merge(window, out, part, lse, o_below, o_above, start, count):
    group = group_of(start, count)
    o_spec = pl.BlockSpec((3 * group, W, HD), lambda s, window: (s, 0, 0))
    stat_spec = pl.BlockSpec((1, W, HD), lambda s, window: (3 * count, 0, 0))
    return pl.pallas_call(
        functools.partial(merge_kernel, start, group),
        grid_spec=pltpu.PrefetchScalarGridSpec(
            num_scalar_prefetch=1,
            grid=(count // group,),
            in_specs=[
                pl.BlockSpec((group, 2, 3, W, HD), lambda s, window: (s, 0, 0, 0, 0)),
                whole((2, 3 * W, HD)),
                o_spec,
                o_spec,
                stat_spec,
                stat_spec,
            ]
            + ([] if out is None else [pl.BlockSpec(memory_space=pl.ANY)]),
            out_specs=heads_spec(start, group),
            scratch_shapes=[pltpu.VMEM((2, 3 * W, HD), F32)],
        ),
        out_shape=jax.ShapeDtypeStruct((2, 3, W, NH * HD), BF16),
        input_output_aliases={} if out is None else {7: 0},
        compiler_params=params(),
        cost_estimate=cost(0.25 * count),
        name="merge",
    )(window, part, lse, o_below, o_above, o_below, o_above, *([] if out is None else [out]))


def exchange(axis, first, second):
    out = []
    for start, block in enumerate((first, second)):
        pairs = [(i, i + 1) for i in range(start, lax.axis_size(axis) - 1, 2)]
        out.append(lax.ppermute(block, axis, pairs + [(b, a) for a, b in pairs]))
    return out


def attention(window, q, k, v, q_gain, k_gain, q_inverse, k_inverse):
    norms = (q_gain, k_gain, q_inverse, k_inverse)
    chunks = ((0, FIRST), (FIRST, NH - FIRST))
    queries, rows = [], []
    for start, count in chunks:
        packed_rows = pack_rows(window, k, v, k_gain, k_inverse, start, count)
        rows.append(exchange("height", *packed_rows))
        q, *_ = lax.optimization_barrier((q, *packed_rows))
        packed = pack_queries(window, q, q_gain, q_inverse, start, count)
        queries.append(exchange("frame", *packed))
        k, *_ = lax.optimization_barrier((k, *packed))
    (start, count), (late_start, late_count) = chunks
    part, *far, lse = both_partial(window, *queries[0], q, k, v, *norms, *rows[0], start, count)
    parts = [(part, lse, *exchange("frame", *far), start, count)]
    far = far_partial(window, queries[1], k, v, k_gain, k_inverse, rows[1], late_start, late_count)
    part, lse = own_partial(window, q, k, v, *norms, rows[1], late_start, late_count)
    parts.append((part, lse, *exchange("frame", *far), late_start, late_count))
    out = None
    for part in parts:
        out = merge(window, out, *part)
    return out


def squares_of(raw):
    values = raw.astype(F32)
    return jnp.sum(values * values, axis=-1)


def body(q, k, v, q_gain, k_gain, window):
    width_total = q.shape[3] * lax.axis_size("head")
    query_sum, key_sum = lax.psum((squares_of(q), squares_of(k)), "head")

    def inverse_of(total):
        return jnp.broadcast_to(lax.rsqrt(total / width_total + EPS)[..., None], (2, 3, W, HD))

    return attention(
        window, q, k, v, q_gain[None], k_gain[None], inverse_of(query_sum), inverse_of(key_sum)
    )


def solution(mesh):
    placed = (
        P("frame", "height", None, "head"),
        P("frame", "height", None, "head"),
        P("frame", "height", None, "head"),
        P("head"),
        P("head"),
        P("head", None),
    )
    return jax.shard_map(
        body,
        mesh=mesh,
        in_specs=placed,
        out_specs=P("frame", "height", None, "head"),
        check_vma=False,
    )
```
